32 devices in a mesh: flow: 2 (over x), col: 4 (over y, core), row: 4 (over z).
Axes of the slice: x: 2, y: 2, z: 4, core: 2. Of those that a mesh axis runs over, the one named last changes fastest.
Arguments:
- forcing: float32 [5, 12, 48, 768], P(None, 'flow', 'col', 'row'), may hold values from -6 to 6
- previous: float32 [5, 12, 48, 768], P(None, 'flow', 'col', 'row'), may hold values from -6 to 6
- element_diagonal_shift: float32 [2, 8, 128], P('flow', 'col', 'row'), may hold values from 0.5 to 4
- eigen_bases: float32 [3, 6, 6], replicated, may hold values from -1 to 1, as said below
- eigen_values: float32 [3, 6], replicated, may hold values from 0.5 to 8
- observers: float32 [3, 256], replicated, may hold values from 8 to 30
- panel_points: float32 [3, 1024], P(None, ('flow', 'col', 'row')), may hold values from -2 to 2
- surface_history: float32 [4, 15, 1024], P(None, None, ('flow', 'col', 'row')), may hold values from -6 to 6
Outputs:
- new_state: float32 [5, 12, 48, 768], P(None, 'flow', 'col', 'row')
- spectra: float32 [2, 16, 256], P(None, None, 'row')
The draws below stay inside these ranges and needn't reach their ends.
Inputs may be any that keep to these rules, and one draw needn't show every extreme that they name: Each eigen_bases[d] is an orthogonal matrix.
All inputs are finite; a program needn't handle non-finite values.
Results may differ from the reference program's by a relative error of at most 0.0003.
Values sent between devices are 32-bit elements; how exact they have to be, the bound alone decides.
A program may use at most 64 MiB of HBM per device.

```python
import math
import jax
import jax.numpy as jnp
from jax import lax

P_SIZE = 6
COMPS = 5
EX = 1
EY = 2
EZ = 32
SWEEPS = 2
ELEMENTS_FIRST = 2
ELEMENTS_SECOND = 8
ELEMENTS_THIRD = 128
NX = 12
NY = 48
NZ = 768
PAN_DEV = 32
PANELS = 1024
NT = 16
NF = 16
OBS = 256
N_FLOW = 2
N_COL = 4
N_ROW = 4


def draw_eigen_bases(key, part):
    size_key, random_sign_key = jax.random.split(jax.random.fold_in(key, 11))
    magnitude = jax.random.uniform(size_key, (3, P_SIZE), jnp.float32, 0.5, 1.5)
    signs = (2 * jax.random.randint(random_sign_key, (3, P_SIZE), 0, 2) - 1).astype(jnp.float32)
    vector = magnitude * signs
    length = jnp.sum(vector * vector, axis=1)
    identity = jnp.eye(P_SIZE, dtype=jnp.float32)
    return identity[None] - 2.0 * vector[:, :, None] * vector[:, None, :] / length[:, None, None]


def levels(rng, shape, cuts, low, top_value):
    gain, own = 1.0, jax.random.fold_in(rng, 6)
    for dim, shards_of in cuts:
        steps = jnp.exp(jax.random.uniform(jax.random.fold_in(own, dim), (shards_of,), jnp.float32, low / len(cuts), top_value / len(cuts)))
        gain = gain * jnp.repeat(steps, shape[dim] // shards_of).reshape([-1 if axis == dim else 1 for axis in range(len(shape))])
    return gain


def centred(key, shape, scale, bound, cuts=(), held_as=jnp.bfloat16):
    entries = scale * jax.random.normal(key, shape, jnp.float32)
    if cuts:
        entries = entries * levels(key, shape, cuts, -0.22, 0.18)
    return jnp.clip(entries, -bound, bound).astype(held_as)


def setup_inputs(seed: int = 0) -> dict:
    key_of = jax.random.split(jax.random.key(seed), 9)
    forcing = centred(key_of[0], (COMPS, NX, NY, NZ), 1.0, 6.0, ((1, 2), (2, 4), (3, 4)), jnp.float32)
    previous = centred(key_of[1], (COMPS, NX, NY, NZ), 1.0, 6.0, ((1, 2), (2, 4), (3, 4)), jnp.float32)
    element_diagonal_shift = jnp.clip(jnp.exp(math.log(4.0) - 2.0794415 * jax.random.uniform(key_of[2], (ELEMENTS_FIRST, ELEMENTS_SECOND, ELEMENTS_THIRD), jnp.float32) ** levels(key_of[2], (ELEMENTS_FIRST, ELEMENTS_SECOND, ELEMENTS_THIRD), ((0, 2), (1, 4), (2, 4)), -0.2, 0.2)), 0.5, 4.0)
    eigen_bases = draw_eigen_bases(jax.random.fold_in(key_of[8], 71), 0)
    eigen_values = jnp.clip(jnp.exp(jax.random.uniform(key_of[4], (3, P_SIZE), jnp.float32, math.log(0.5), math.log(8.0))), 0.5, 8.0)
    observers = jnp.clip(jax.random.uniform(key_of[5], (3, OBS), jnp.float32, 8.0, 30.0), 8.0, 30.0)
    panel_points = jnp.clip(jax.random.uniform(key_of[6], (3, PANELS), jnp.float32, -2.0, 2.0) * levels(key_of[6], (3, PANELS), ((1, 32),), -0.4, 0.0), -2.0, 2.0)
    surface_history = centred(key_of[7], (4, NT - 1, PANELS), 1.0, 6.0, ((2, 32),), jnp.float32)
    return dict(forcing=forcing, previous=previous, element_diagonal_shift=element_diagonal_shift, eigen_bases=eigen_bases, eigen_values=eigen_values, observers=observers, panel_points=panel_points, surface_history=surface_history)


HIGH = lax.Precision.HIGHEST
OMEGA = 0.8
TAU = 0.5
KMAX = 2.0

def contract(field, matrix, which):
    extent = field.shape
    count = extent[which]
    blocked = field.reshape(extent[:which] + (count // P_SIZE, P_SIZE) + extent[which + 1:])
    blocked = jnp.moveaxis(blocked, which + 1, -1)
    result = jnp.einsum('...p,qp->...q', blocked, matrix, precision=HIGH)
    result = jnp.moveaxis(result, -1, which + 1)
    return result.reshape(extent)

def face_masks(count):
    index = jnp.arange(count) % P_SIZE
    return ((index == P_SIZE - 1).astype(jnp.float32), (index == 0).astype(jnp.float32))

def far_terms(observers, points, source_re, source_im):
    offsets = observers[:, :, None] - points[:, None, :]
    radius = jnp.sqrt(lax.optimization_barrier(jnp.sum(offsets * offsets, axis=0)))
    unit_dir = offsets / radius[None]
    freqs = source_re.shape[1]
    wavenum = (KMAX * (jnp.arange(freqs, dtype=jnp.float32) + 0.5) / freqs)[:, None, None]
    along_re = unit_dir[0][None] * source_re[1][:, None, :] + unit_dir[1][None] * source_re[2][:, None, :] + unit_dir[2][None] * source_re[3][:, None, :]
    along_im = unit_dir[0][None] * source_im[1][:, None, :] + unit_dir[1][None] * source_im[2][:, None, :] + unit_dir[2][None] * source_im[3][:, None, :]
    inverse_matrix = 1.0 / radius[None]
    term_re = -wavenum * (source_im[0][:, None, :] + along_im) + along_re * inverse_matrix
    term_im = wavenum * (source_re[0][:, None, :] + along_re) + along_im * inverse_matrix
    phases = wavenum * radius[None]
    amplitude = inverse_matrix / (4.0 * math.pi)
    green_re = amplitude * jnp.cos(phases)
    green_im = -amplitude * jnp.sin(phases)
    total_re = lax.optimization_barrier(jnp.sum(green_re * term_re - green_im * term_im, axis=2))
    total_im = lax.optimization_barrier(jnp.sum(green_re * term_im + green_im * term_re, axis=2))
    return jnp.stack([total_re, total_im])

def reference(forcing, previous, element_diagonal_shift, eigen_bases, eigen_values, observers, panel_points, surface_history):
    stiffness = [jnp.dot(eigen_bases[axis_num] * eigen_values[axis_num][None, :], eigen_bases[axis_num].T, precision=HIGH) for axis_num in range(3)]
    shift_nodes = jnp.repeat(jnp.repeat(jnp.repeat(element_diagonal_shift, P_SIZE, 0), P_SIZE, 1), P_SIZE, 2)
    denominator = shift_nodes + jnp.tile(eigen_values[0], NX // P_SIZE)[:, None, None] + jnp.tile(eigen_values[1], NY // P_SIZE)[None, :, None] + jnp.tile(eigen_values[2], NZ // P_SIZE)[None, None, :]
    high_x, low_x = face_masks(NX)
    high_y, low_y = face_masks(NY)
    high_z, low_z = face_masks(NZ)

    def apply_block(field):
        result = shift_nodes[None] * field
        for axis_num in range(3):
            result = result + contract(field, stiffness[axis_num], axis_num + 1)
        return result

    def block_inverse(field):
        result = field
        for axis_num in range(3):
            result = contract(result, eigen_bases[axis_num].T, axis_num + 1)
        result = result / denominator[None]
        for axis_num in range(3):
            result = contract(result, eigen_bases[axis_num], axis_num + 1)
        return result

    def coupling(field):
        padded = jnp.pad(field, ((0, 0), (1, 1), (1, 1), (1, 1)))
        result = high_x[None, :, None, None] * padded[:, 2:, 1:-1, 1:-1] + low_x[None, :, None, None] * padded[:, :-2, 1:-1, 1:-1]
        result = result + high_y[None, None, :, None] * padded[:, 1:-1, 2:, 1:-1] + low_y[None, None, :, None] * padded[:, 1:-1, :-2, 1:-1]
        result = result + high_z[None, None, None, :] * padded[:, 1:-1, 1:-1, 2:] + low_z[None, None, None, :] * padded[:, 1:-1, 1:-1, :-2]
        return result
    state = previous
    for sweep in range(SWEEPS):
        residual = forcing - apply_block(state) + TAU * coupling(state)
        state = state + OMEGA * block_inverse(residual)
    corner = state[:4, ::EX * P_SIZE, ::EY * P_SIZE, :]
    corner = corner.reshape(4, N_FLOW, N_COL, N_ROW, EZ * P_SIZE)[:, :, :, :, :PAN_DEV]
    newest = corner.reshape(4, PANELS)
    surface_samples = jnp.concatenate([surface_history, newest[:, None, :]], axis=1)
    times = jnp.arange(NT, dtype=jnp.float32)
    omegas = math.pi * (jnp.arange(NF, dtype=jnp.float32) + 0.5) / NF
    cos_table = jnp.cos(omegas[:, None] * times[None, :])
    sin_table = jnp.sin(omegas[:, None] * times[None, :])
    source_re = jnp.einsum('fn,cnp->cfp', cos_table, surface_samples, precision=HIGH)
    source_im = -jnp.einsum('fn,cnp->cfp', sin_table, surface_samples, precision=HIGH)
    block_len = math.gcd(PANELS, 1024)
    block_count = PANELS // block_len
    point_blocks = panel_points.reshape(3, block_count, block_len).transpose(1, 0, 2)
    re_blocks = source_re.reshape(4, NF, block_count, block_len).transpose(2, 0, 1, 3)
    imaginary_blocks = source_im.reshape(4, NF, block_count, block_len).transpose(2, 0, 1, 3)

    def add_block(total, pieces):
        return (total + far_terms(observers, pieces[0], pieces[1], pieces[2]), None)
    spectra, unused = lax.scan(add_block, jnp.zeros((2, NF, OBS), jnp.float32), (point_blocks, re_blocks, imaginary_blocks))
    return (state, spectra)
```

```python
import functools
import math

import jax
import jax.numpy as jnp
from jax import lax
from jax.experimental import pallas as pl
from jax.experimental.pallas import tpu as pltpu
from jax.sharding import PartitionSpec as P

N = 6
SWEEPS = 2
NT = 16
NF = 16
OMEGA = 0.8
TAU = 0.5
KMAX = 2.0
BLK = 256
HIGH = lax.Precision.HIGHEST
MESH = pl.DeviceIdType.MESH
F32 = jnp.float32
NN = (((1,), (0,)), ((), ()))
NTD = (((1,), (1,)), ((), ()))


def ddot(a, b, dims=NN):
    return lax.dot_general(a, b, dims, precision=HIGH, preferred_element_type=F32)


def split(a):
    hi = a.astype(jnp.bfloat16)
    return hi, (a - hi.astype(F32)).astype(jnp.bfloat16)


def dot3(a, b):
    f = functools.partial(lax.dot_general, dimension_numbers=NN, preferred_element_type=F32)
    return f(a[0], b[0]) + (f(a[0], b[1]) + f(a[1], b[0]))


def rows_of(n):
    return lax.broadcasted_iota(jnp.int32, (n, 1), 0).astype(F32)


def cols_of(n):
    return lax.broadcasted_iota(jnp.int32, (1, n), 1).astype(F32)


def divmod_of(v, n):
    q = jnp.floor((v + 0.5) * (1.0 / n))
    return q, v - n * q


def where01(cond):
    return jnp.where(cond, 1.0, 0.0).astype(F32)


def pick(m, r, c, transposed=False):
    left = ddot(where01(r == cols_of(N)), m, NTD if transposed else NN)
    return ddot(left, where01(rows_of(N) == c))


def kernel(
    sizes, f_hbm, u_hbm, lam_ref, bases_ref, vals_ref, obs_ref, pts_ref, hist_ref,
    out_hbm, spec_ref,
    f_in, u_in, out_buf, u_s, f_s, r_s, trace_s, zsend_s, halo_r, z_r,
    pan_s, pan_r, new_s, new_r, er_s, ei_s, part_s, part_r,
    local_sem, hs_sem, hr_sem, ps_sem, pr_sem, ns_sem, nr_sem, ss_sem, sr_sem,
):
    n_flow, n_col, n_row, comps, nx, ny, nz, pan, n_obs = sizes
    ey = ny // N
    nh = nx * ny
    own_obs = n_obs // n_row
    flow, col, row = (lax.axis_index(a) for a in ("flow", "col", "row"))
    n_fc = n_flow * n_col
    fc = flow * n_col + col

    def fc_peer(d):
        t = lax.rem(fc + d, n_fc)
        return (lax.div(t, n_col), lax.rem(t, n_col), row)

    def row_peer(d):
        return (flow, col, lax.rem(row + d, n_row))

    def each_fc(body):
        if n_fc <= 16:
            for d in range(1, n_fc):
                body(d)
        else:
            lax.fori_loop(1, n_fc, lambda d, c: (body(d), c)[1], 0)

    u_copy = pltpu.make_async_copy(u_hbm, u_in, local_sem.at[0])
    f_copy = pltpu.make_async_copy(f_hbm, f_in, local_sem.at[1])
    u_copy.start()
    f_copy.start()
    halo_r[...] = jnp.zeros(halo_r.shape, F32)
    z_r[...] = jnp.zeros(z_r.shape, F32)
    barrier = pltpu.get_barrier_semaphore()
    each_fc(lambda d: pl.semaphore_signal(barrier, inc=1, device_id=fc_peer(d), device_id_type=MESH))
    for d in range(1, n_row):
        pl.semaphore_signal(barrier, inc=1, device_id=row_peer(d), device_id_type=MESH)

    place = where01(cols_of(128) == rows_of(pan) + (row * pan).astype(F32))
    pan_s[...] = jnp.zeros(pan_s.shape, F32)
    for c in range(4):
        pan_s[c * 16 : c * 16 + NT - 1, :] = ddot(hist_ref[c], place)
    pan_s[64:67, :] = ddot(pts_ref[...], place)

    sx, sy, sz = bases_ref[0], bases_ref[1], bases_ref[2]

    def ends(m, labels, is_row):
        if is_row:
            one = where01(rows_of(N) == labels)
            both = ddot(m, one)
            return both[0:1], both[N - 1 : N]
        one = where01(labels == cols_of(N))
        return (
            jnp.sum(one * m[0:1], axis=1, keepdims=True),
            jnp.sum(one * m[N - 1 : N], axis=1, keepdims=True),
        )

    hr = rows_of(nh)
    hc = cols_of(nh)
    ir, yr = divmod_of(hr, ny)
    er, jr = divmod_of(yr, N)
    ic, yc = divmod_of(hc, ny)
    ec, jc = divmod_of(yc, N)
    x0r, x5r = ends(sx, ic, True)
    y0r, y5r = ends(sy, jc, True)
    x0c, x5c = ends(sx, ir, False)
    y0c, y5c = ends(sy, jr, False)

    def spread(count, period):
        return divmod_of(count, period)

    nc, myc = divmod_of(cols_of(nx * 16), 16)
    mec, mjc = divmod_of(myc, N)
    nr, myr = divmod_of(rows_of(nx * 16), 16)
    mer, mjr = divmod_of(myr, N)
    a_fwd = pick(sx, ir, nc, True) * pick(sy, jr, mjc, True) * where01((er == mec) & (myc < ny))
    zqr, zkr = divmod_of(rows_of(BLK), N)
    zqc, zkc = divmod_of(cols_of(BLK), N)
    zqn, zkn = divmod_of(rows_of(nz), N)
    z_fwd = pick(sz, zkn, zkc) * where01(zqn == zqc)
    a_fwd = split(a_fwd)
    z_fwd = split(z_fwd)

    z0r, z5r = ends(sz, zkc, True)
    z0c, z5c = ends(sz, zkr, False)
    lane = cols_of(BLK)
    ez = nz // N
    inside = lane < nz
    kz = where01((zqr == zqc + 1) & inside & (rows_of(BLK) < nz)) * z0c * z5r
    kz = kz + where01((zqr == zqc - 1) & inside) * z5c * z0r
    first_lane = (lane >= nz) & (lane < nz + comps)
    last_lane = (lane >= nz + 8) & (lane < nz + 8 + comps)
    kz = kz + where01((zqr == 0) & first_lane) * z0c + where01((zqr == ez - 1) & last_lane) * z5c
    kz = split(kz)

    ky = where01(ir == ic) * (
        where01(ec == er + 1) * y5c * y0r + where01(ec == er - 1) * y0c * y5r
    )
    t16, t8 = rows_of(16), rows_of(8)
    mxy = jnp.concatenate(
        [
            ky,
            where01(t16 == yc) * x0r,
            where01(t16 == yc) * x5r,
            where01((t8 == ic) & (ec == 0)) * y0r,
            where01((t8 == ic) & (ec == ey - 1)) * y5r,
        ],
        axis=0,
    )
    mxy = split(mxy)
    hl = cols_of(48)
    inj = where01(hl == yr) * x5c + where01(hl == yr + 16) * x0c
    inj = inj + where01((hl == ir + 32) & (er == ey - 1)) * y5c
    inj = inj + where01((hl == ir + 40) & (er == 0)) * y0c
    inj = split(inj)
    zin5 = jnp.where(zqc == ez - 1, z5r, 0.0)[:, 128:256]
    zin0 = jnp.where(zqc == 0, z0r, 0.0)[:, 0:128]

    pl.semaphore_wait(barrier, (n_fc - 1) + (n_row - 1))

    def pan_copy(d):
        return pltpu.make_async_remote_copy(
            src_ref=pan_s, dst_ref=pan_r.at[d], send_sem=ps_sem.at[d], recv_sem=pr_sem.at[d],
            device_id=row_peer(d), device_id_type=MESH)

    def new_copy(d):
        return pltpu.make_async_remote_copy(
            src_ref=new_s, dst_ref=new_r.at[d], send_sem=ns_sem.at[d], recv_sem=nr_sem.at[d],
            device_id=row_peer(d), device_id_type=MESH)

    def part_copy(d):
        return pltpu.make_async_remote_copy(
            src_ref=part_s, dst_ref=part_r.at[fc], send_sem=ss_sem.at[d], recv_sem=sr_sem.at[d],
            device_id=fc_peer(d), device_id_type=MESH)

    def part_wait(d):
        src = lax.rem(fc + (n_fc - d), n_fc)
        pltpu.make_async_remote_copy(
            src_ref=part_s, dst_ref=part_r.at[src], send_sem=ss_sem.at[d], recv_sem=sr_sem.at[d],
            device_id=fc_peer(d), device_id_type=MESH).wait_recv()

    def faces(s):
        def copy(k, src, dst, where):
            return pltpu.make_async_remote_copy(
                src_ref=src, dst_ref=dst, send_sem=hs_sem.at[s, k], recv_sem=hr_sem.at[s, k],
                device_id=where, device_id_type=MESH)

        def rows(buf, a, n):
            return buf.at[s, pl.ds(a, n), :]

        return (
            (flow > 0, flow < n_flow - 1, copy(0, rows(trace_s, 0, 16), rows(halo_r, 0, 16), (flow - 1, col, row))),
            (flow < n_flow - 1, flow > 0, copy(1, rows(trace_s, 16, 16), rows(halo_r, 16, 16), (flow + 1, col, row))),
            (col > 0, col < n_col - 1, copy(2, rows(trace_s, 32, 8), rows(halo_r, 32, 8), (flow, col - 1, row))),
            (col < n_col - 1, col > 0, copy(3, rows(trace_s, 40, 8), rows(halo_r, 40, 8), (flow, col + 1, row))),
            (row > 0, row < n_row - 1, copy(4, zsend_s.at[s], z_r.at[s, 0], (flow, col, row - 1))),
            (row < n_row - 1, row > 0, copy(5, zsend_s.at[s], z_r.at[s, 1], (flow, col, row + 1))),
        )

    def forward(ref):
        parts = []
        for c in range(comps):
            fill = jnp.zeros((16 - ny, nz), F32)
            x = jnp.concatenate([p for i in range(nx) for p in (ref[c, i], fill)], axis=0)
            y = dot3(split(x), z_fwd)
            parts.append(dot3(a_fwd, split(y)))
        return parts

    def couple(parts, s):
        acc = None
        inner = []
        for c in range(comps):
            u = split(parts[c])
            w = dot3(u, kz)
            t = dot3(mxy, u)
            trace_s[s, :, c * BLK : (c + 1) * BLK] = t[nh : nh + 48]
            lanes = cols_of(128)
            keep = (lanes == nz - 128 + c) | (lanes == nz - 120 + c)
            piece = jnp.where(keep, w[:, 128:256], 0.0)
            acc = piece if acc is None else acc + piece
            inner.append(w + t[:nh])
        zsend_s[s] = acc
        for sends, _, copy in faces(s):
            pl.when(sends)(copy.start)
        return inner

    def finish(s):
        for _, receives, copy in faces(s):
            pl.when(receives)(copy.wait_recv)

    def update(parts, inner, s):
        zn, zp = z_r[s, 0], z_r[s, 1]
        r = r_s[...]
        new = []
        for c in range(comps):
            add = dot3(inj, split(halo_r[s, :, c * BLK : (c + 1) * BLK]))
            zlo = zp[:, nz - 120 + c : nz - 119 + c] * zin0
            zhi = zn[:, nz - 128 + c : nz - 127 + c] * zin5
            total = inner[c] + add + jnp.concatenate([zlo, zhi], axis=1)
            new.append((1.0 - OMEGA) * parts[c] + r * (f_s[c] + TAU * total))
        return new

    u_copy.wait()
    state = forward(u_in)
    inner = couple(state, 0)
    for c in range(comps):
        u_s[c] = state[c]
    for d in range(1, n_row):
        pan_copy(d).start()

    f_copy.wait()
    for c, part in enumerate(forward(f_in)):
        f_s[c] = part
    lam = ddot(ddot(where01(er == cols_of(ey)), lam_ref[0]), where01(rows_of(ez) == zqc))
    onx = jnp.sum(where01(ir == cols_of(N)) * vals_ref[0:1, :], axis=1, keepdims=True)
    ony = jnp.sum(where01(jr == cols_of(N)) * vals_ref[1:2, :], axis=1, keepdims=True)
    onz = ddot(vals_ref[...], where01(rows_of(N) == zkc))[2:3]
    r_s[...] = jnp.where(inside, OMEGA / jnp.where(inside, lam + onx + ony + onz, 1.0), 0.0)

    finish(0)
    state = update([u_s[c] for c in range(comps)], inner, 0)
    inner = couple(state, 1)
    for c in range(comps):
        u_s[c] = state[c]

    for d in range(1, n_row):
        pan_copy(d).wait_recv()
    panels = pan_s[...]
    for d in range(1, n_row):
        panels = panels + pan_r[d]
    own = where01(cols_of(n_obs) == rows_of(own_obs) + (row * own_obs).astype(F32))
    mine = ddot(own, obs_ref[...], NTD)
    dx, dy, dz = (mine[:, a : a + 1] - panels[64 + a : 65 + a, :] for a in range(3))
    r2 = dx * dx + dy * dy + dz * dz
    radius = jnp.sqrt(r2)
    inv = 1.0 / radius
    dx, dy, dz = dx * inv, dy * inv, dz * inv
    amp = inv * (1.0 / (4.0 * math.pi))
    step = KMAX / NF
    ar, ai = jnp.cos(radius * (0.5 * step)), -jnp.sin(radius * (0.5 * step))
    sr, si = ar * ar - ai * ai, 2.0 * ar * ai
    ar, ai = ar * amp, ai * amp
    angle = (rows_of(NF) + 0.5) * (math.pi / NF) * cols_of(NT)
    cos_t, sin_t = jnp.cos(angle), -jnp.sin(angle)
    both_t = jnp.concatenate([cos_t, sin_t], axis=0)
    q = [ddot(both_t, panels[c * 16 : (c + 1) * 16, :]) for c in range(4)]
    lane128 = lax.broadcasted_iota(jnp.int32, (1, 128), 1)
    total = jnp.zeros((own_obs, 128), F32)
    for f in range(NF):
        k = step * (f + 0.5)
        er_s[f], ei_s[f] = ar, ai
        re, im = [x[f : f + 1] for x in q], [x[NF + f : NF + f + 1] for x in q]
        d_re = dx * re[1] + dy * re[2] + dz * re[3]
        d_im = dx * im[1] + dy * im[2] + dz * im[3]
        t_re = d_re * inv - k * (im[0] + d_im)
        t_im = d_im * inv + k * (re[0] + d_re)
        s_re = jnp.sum(ar * t_re - ai * t_im, axis=1, keepdims=True)
        s_im = jnp.sum(ar * t_im + ai * t_re, axis=1, keepdims=True)
        total = jnp.where(lane128 == f, s_re, total)
        total = jnp.where(lane128 == NF + f, s_im, total)
        if f < NF - 1:
            ar, ai = ar * sr - ai * si, ar * si + ai * sr

    a_back = pick(sx, nr, ic) * pick(sy, mjr, jc) * where01((mer == ec) & (myr < ny))
    a_back = split(a_back)
    zq_own, zk_own = divmod_of(cols_of(nz), N)
    z_back = split(pick(sz, zkr, zk_own, True) * where01(zqr == zq_own))
    zs = cols_of(128) - (row * pan).astype(F32)
    sq, sk = divmod_of(zs, N)
    z_new = pick(sz, zkr, sk, True) * where01((zqr == sq) & (zs >= 0) & (zs < pan))
    z_new = split(z_new)
    last_re = jnp.sum(jnp.where(cols_of(NT) == NT - 1, both_t, 0.0), axis=1, keepdims=True)

    finish(1)
    state = update([u_s[c] for c in range(comps)], inner, 1)
    corner = (a_back[0][0:16], a_back[1][0:16])
    eight = rows_of(8)
    corners = jnp.zeros((8, BLK), F32)
    halves = [split(s) for s in state]
    for c in range(4):
        corners = jnp.where(eight == c, dot3(corner, halves[c])[0:1], corners)
    new_s[...] = dot3(split(corners), z_new)
    for d in range(1, n_row):
        new_copy(d).start()

    for c in range(comps):
        w = dot3(halves[c], z_back)
        nodes = dot3(a_back, split(w))
        for i in range(nx):
            out_buf[c, i] = nodes[i * 16 : i * 16 + ny]
    out_copy = pltpu.make_async_copy(out_buf, out_hbm, local_sem.at[2])
    out_copy.start()

    for d in range(1, n_row):
        new_copy(d).wait_recv()
    newest = new_s[...]
    for d in range(1, n_row):
        newest = newest + new_r[d]
    along = dx * newest[1:2] + dy * newest[2:3] + dz * newest[3:4]
    a_val = newest[0:1] + along
    b_val = along * inv
    fresh = jnp.zeros((own_obs, 128), F32)
    for f in range(NF):
        k = step * (f + 0.5)
        ka = k * a_val
        gr, gi = er_s[f], ei_s[f]
        s_re = jnp.sum(gr * b_val - gi * ka, axis=1, keepdims=True)
        s_im = jnp.sum(gr * ka + gi * b_val, axis=1, keepdims=True)
        fresh = jnp.where(lane128 == f, s_re, fresh)
        fresh = jnp.where(lane128 == NF + f, s_im, fresh)
    turned = jnp.concatenate([fresh, total], axis=0).T
    fr, fi = turned[0:NF], turned[NF : 2 * NF]
    c15, s15 = last_re[0:NF], last_re[NF : 2 * NF]
    now_re = c15 * fr - s15 * fi
    now_im = c15 * fi + s15 * fr
    part_s[0:NF, :] = now_re + pltpu.roll(fr, own_obs, 1)
    part_s[NF : 2 * NF, :] = now_im + pltpu.roll(fi, own_obs, 1)
    part_r[fc] = part_s[...]
    each_fc(lambda d: part_copy(d).start())
    each_fc(part_wait)
    if n_fc <= 16:
        spectra = part_r[0]
        for d in range(1, n_fc):
            spectra = spectra + part_r[d]
    else:
        spectra = lax.fori_loop(1, n_fc, lambda d, acc: acc + part_r[d], part_r[0])
    spec_ref[0] = spectra[0:NF, :own_obs]
    spec_ref[1] = spectra[NF : 2 * NF, :own_obs]

    for s in range(SWEEPS):
        for sends, _, copy in faces(s):
            pl.when(sends)(copy.wait_send)
    for d in range(1, n_row):
        pan_copy(d).wait_send()
        new_copy(d).wait_send()
    each_fc(lambda d: part_copy(d).wait_send())
    out_copy.wait()


def on_device(forcing, previous, shift, bases, values, observers, points, history):
    n_flow, n_col, n_row = (lax.axis_size(a) for a in ("flow", "col", "row"))
    comps, nx, ny, nz = forcing.shape
    n_fc = n_flow * n_col
    pan = points.shape[1]
    n_obs = observers.shape[1]
    own_obs = n_obs // n_row
    nh = nx * ny
    sizes = (n_flow, n_col, n_row, comps, nx, ny, nz, pan, n_obs)
    vmem = pl.BlockSpec(memory_space=pltpu.VMEM)
    hbm = pl.BlockSpec(memory_space=pl.ANY)
    dma = pltpu.SemaphoreType.DMA
    return pl.pallas_call(
        functools.partial(kernel, sizes),
        out_shape=(
            jax.ShapeDtypeStruct(forcing.shape, F32),
            jax.ShapeDtypeStruct((2, NF, own_obs), F32),
        ),
        in_specs=[hbm, hbm] + [vmem] * 6,
        out_specs=(hbm, vmem),
        scratch_shapes=[
            pltpu.VMEM((comps, nx, ny, nz), F32),
            pltpu.VMEM((comps, nx, ny, nz), F32),
            pltpu.VMEM((comps, nx, ny, nz), F32),
            pltpu.VMEM((comps, nh, BLK), F32),
            pltpu.VMEM((comps, nh, BLK), F32),
            pltpu.VMEM((nh, BLK), F32),
            pltpu.VMEM((SWEEPS, 48, comps * BLK), F32),
            pltpu.VMEM((SWEEPS, nh, 128), F32),
            pltpu.VMEM((SWEEPS, 48, comps * BLK), F32),
            pltpu.VMEM((SWEEPS, 2, nh, 128), F32),
            pltpu.VMEM((72, 128), F32),
            pltpu.VMEM((n_row, 72, 128), F32),
            pltpu.VMEM((8, 128), F32),
            pltpu.VMEM((n_row, 8, 128), F32),
            pltpu.VMEM((NF, own_obs, 128), F32),
            pltpu.VMEM((NF, own_obs, 128), F32),
            pltpu.VMEM((2 * NF, 128), F32),
            pltpu.VMEM((n_fc, 2 * NF, 128), F32),
            dma((3,)),
            dma((SWEEPS, 6)),
            dma((SWEEPS, 6)),
            dma((n_row,)),
            dma((n_row,)),
            dma((n_row,)),
            dma((n_row,)),
            dma((n_fc,)),
            dma((n_fc,)),
        ],
        compiler_params=pltpu.CompilerParams(
            collective_id=0, has_side_effects=True, vmem_limit_bytes=48 * 1024 * 1024
        ),
    )(forcing, previous, shift, bases, values, observers, points, history)


def solution(mesh):
    return jax.shard_map(
        on_device,
        mesh=mesh,
        in_specs=(
            P(None, "flow", "col", "row"),
            P(None, "flow", "col", "row"),
            P("flow", "col", "row"),
            P(),
            P(),
            P(),
            P(None, ("flow", "col", "row")),
            P(None, None, ("flow", "col", "row")),
        ),
        out_specs=(P(None, "flow", "col", "row"), P(None, None, "row")),
        check_vma=False,
    )
```

```python
import functools
import math

import jax
import jax.numpy as jnp
from jax import lax
from jax.experimental import pallas as pl
from jax.experimental.pallas import tpu as pltpu
from jax.sharding import PartitionSpec as P

N = 6
SWEEPS = 2
NT = 16
NF = 16
OMEGA = 0.8
TAU = 0.5
KMAX = 2.0
BLK = 256
HIGH = lax.Precision.HIGHEST
MESH = pl.DeviceIdType.MESH
F32 = jnp.float32
BF16 = jnp.bfloat16
NN = (((1,), (0,)), ((), ()))
NTD = (((1,), (1,)), ((), ()))


def ddot(a, b, dims=NN):
    return lax.dot_general(a, b, dims, precision=HIGH, preferred_element_type=F32)


def bdot(a, b, dims=NN):
    return lax.dot_general(a, b, dims, preferred_element_type=F32)


def split(a):
    hi = a.astype(BF16)
    return hi, (a - hi.astype(F32)).astype(BF16)


def left3(a):
    hi, lo = split(a)
    return jnp.concatenate([hi, lo, hi], axis=1)


def right3(b):
    hi, lo = split(b)
    return jnp.concatenate([hi, hi, lo], axis=0)


def rows_of(n):
    return lax.broadcasted_iota(jnp.int32, (n, 1), 0).astype(F32)


def cols_of(n):
    return lax.broadcasted_iota(jnp.int32, (1, n), 1).astype(F32)


def divmod_of(v, n):
    q = jnp.floor((v + 0.5) * (1.0 / n))
    return q, v - n * q


def where01(cond):
    return jnp.where(cond, 1.0, 0.0).astype(F32)


def pick(m, r, c, transposed=False):
    on_r = where01(r == cols_of(N)).astype(BF16)
    on_c = where01(rows_of(N) == c).astype(BF16)
    total = None
    for part in split(m):
        left = bdot(on_r, part, NTD if transposed else NN).astype(BF16)
        out = bdot(left, on_c)
        total = out if total is None else total + out
    return total


def lookup(row, labels):
    total = None
    for k in range(N):
        term = row[:, k : k + 1] * where01(labels == k)
        total = term if total is None else total + term
    return total


def sincos(x):
    n = jnp.floor(x * (2.0 / math.pi) + 0.5)
    y = ((x - n * 1.5703125) - n * 4.83751296997e-4) - n * 7.54978995489e-8
    z = y * y
    s = y + y * z * (-1.6666654611e-1 + z * (8.3321608736e-3 - z * 1.9515295891e-4))
    c = 1.0 - 0.5 * z + z * z * (4.166664568298827e-2 - z * (1.388731625493765e-3 - z * 2.443315711809948e-5))
    q = n - 4.0 * jnp.floor(n * 0.25)
    odd = (q == 1.0) | (q == 3.0)
    sin = jnp.where(odd, c, s) * jnp.where(q >= 2.0, -1.0, 1.0)
    cos = jnp.where(odd, s, c) * jnp.where((q == 1.0) | (q == 2.0), -1.0, 1.0)
    return sin, cos


def kernel(
    sizes, f_hbm, u_hbm, lam_hbm, bases_hbm, vals_hbm, obs_hbm, pts_hbm, hist_hbm,
    out_hbm, spec_ref,
    f_in, u_in, lam_ref, bases_ref, vals_ref, obs_ref, pts_ref, hist_ref,
    out_buf, u_s, f_s, r_s, trace_s, zsend_s, halo_r, z_r,
    pan_s, pan_r, new_s, new_r, er_s, ei_s, part_s, part_r,
    local_sem, hs_sem, hr_sem, ps_sem, pr_sem, ns_sem, nr_sem, ss_sem, sr_sem,
):
    n_flow, n_col, n_row, comps, nx, ny, nz, pan, n_obs, nh = sizes
    ey, ez = ny // N, nz // N
    own_obs = n_obs // n_row
    flow, col, row = (lax.axis_index(a) for a in ("flow", "col", "row"))
    n_fc = n_flow * n_col
    fc = flow * n_col + col

    def fc_peer(d):
        t = lax.rem(fc + d, n_fc)
        return (lax.div(t, n_col), lax.rem(t, n_col), row)

    def row_peer(d):
        return (flow, col, lax.rem(row + d, n_row))

    def each_fc(body):
        if n_fc <= 16:
            for d in range(1, n_fc):
                body(d)
        else:
            lax.fori_loop(1, n_fc, lambda d, c: (body(d), c)[1], 0)

    pairs = (
        (bases_hbm, bases_ref), (u_hbm, u_in), (pts_hbm, pts_ref), (hist_hbm, hist_ref),
        (f_hbm, f_in), (lam_hbm, lam_ref), (vals_hbm, vals_ref), (obs_hbm, obs_ref),
    )
    local = [pltpu.make_async_copy(a, b, local_sem.at[i]) for i, (a, b) in enumerate(pairs)]
    for copy in local:
        copy.start()
    halo_r[...] = jnp.zeros(halo_r.shape, F32)
    z_r[...] = jnp.zeros(z_r.shape, F32)
    barrier = pltpu.get_barrier_semaphore()
    each_fc(lambda d: pl.semaphore_signal(barrier, inc=1, device_id=fc_peer(d), device_id_type=MESH))
    for d in range(1, n_row):
        pl.semaphore_signal(barrier, inc=1, device_id=row_peer(d), device_id_type=MESH)

    local[0].wait()
    sx, sy, sz = bases_ref[0], bases_ref[1], bases_ref[2]

    def ends(m, labels):
        return lookup(m[0:1], labels), lookup(m[N - 1 : N], labels)

    hr = rows_of(nh)
    hc = cols_of(nh)
    ir, yr = divmod_of(hr, ny)
    er, jr = divmod_of(yr, N)
    ic, yc = divmod_of(hc, ny)
    ec, jc = divmod_of(yc, N)
    x0r, x5r = ends(sx, ic)
    y0r, y5r = ends(sy, jc)
    x0c, x5c = ends(sx, ir)
    y0c, y5c = ends(sy, jr)

    nc, myc = divmod_of(cols_of(nx * 16), 16)
    mec, mjc = divmod_of(myc, N)
    nr, myr = divmod_of(rows_of(nx * 16), 16)
    mer, mjr = divmod_of(myr, N)
    a_fwd = pick(sx, ir, nc, True) * pick(sy, jr, mjc, True) * where01((er == mec) & (myc < ny))
    lane = cols_of(BLK)
    inside = lane < nz
    zqr, zkr = divmod_of(rows_of(BLK), N)
    zqc, zkc = divmod_of(lane, N)
    z_fwd = pick(sz, zkr, zkc) * where01((zqr == zqc) & inside)
    a_fwd = left3(a_fwd)
    z_fwd = right3(z_fwd)

    z0r, z5r = ends(sz, zkc)
    z0c, z5c = ends(sz, zkr)
    kz = where01((zqr == zqc + 1) & inside & (zqr < ez)) * z0c * z5r
    kz = kz + where01((zqr == zqc - 1) & inside) * z5c * z0r
    first_lane = (lane >= nz) & (lane < nz + comps)
    last_lane = (lane >= nz + 8) & (lane < nz + 8 + comps)
    kz = kz + where01((zqr == 0) & first_lane) * z0c + where01((zqr == ez - 1) & last_lane) * z5c
    kz = right3(kz)

    ky = where01(ir == ic) * (
        where01(ec == er + 1) * y5c * y0r + where01(ec == er - 1) * y0c * y5r
    )
    t16, t8 = rows_of(16), rows_of(8)
    mxy = jnp.concatenate(
        [
            ky,
            where01(t16 == yc) * x0r,
            where01(t16 == yc) * x5r,
            where01((t8 == ic) & (ec == 0)) * y0r,
            where01((t8 == ic) & (ec == ey - 1)) * y5r,
        ],
        axis=0,
    )
    mxy = left3(mxy)
    hl = cols_of(48)
    inj = where01(hl == yr) * x5c + where01(hl == yr + 16) * x0c
    inj = inj + where01((hl == ir + 32) & (er == ey - 1)) * y5c
    inj = inj + where01((hl == ir + 40) & (er == 0)) * y0c
    inj = left3(inj)
    zin5 = jnp.where(zqc == ez - 1, z5r, 0.0)[:, 128:256]
    zin0 = jnp.where(zqc == 0, z0r, 0.0)[:, 0:128]

    def pan_copy(d):
        return pltpu.make_async_remote_copy(
            src_ref=pan_s, dst_ref=pan_r.at[d], send_sem=ps_sem.at[d], recv_sem=pr_sem.at[d],
            device_id=row_peer(d), device_id_type=MESH)

    def new_copy(d):
        return pltpu.make_async_remote_copy(
            src_ref=new_s, dst_ref=new_r.at[d], send_sem=ns_sem.at[d], recv_sem=nr_sem.at[d],
            device_id=row_peer(d), device_id_type=MESH)

    def part_copy(d):
        return pltpu.make_async_remote_copy(
            src_ref=part_s, dst_ref=part_r.at[fc], send_sem=ss_sem.at[d], recv_sem=sr_sem.at[d],
            device_id=fc_peer(d), device_id_type=MESH)

    def part_wait(d):
        src = lax.rem(fc + (n_fc - d), n_fc)
        pltpu.make_async_remote_copy(
            src_ref=part_s, dst_ref=part_r.at[src], send_sem=ss_sem.at[d], recv_sem=sr_sem.at[d],
            device_id=fc_peer(d), device_id_type=MESH).wait_recv()

    def faces(s):
        def copy(k, src, dst, where):
            return pltpu.make_async_remote_copy(
                src_ref=src, dst_ref=dst, send_sem=hs_sem.at[s, k], recv_sem=hr_sem.at[s, k],
                device_id=where, device_id_type=MESH)

        def rows(buf, a, n):
            return buf.at[s, pl.ds(a, n), :]

        return (
            (flow > 0, flow < n_flow - 1, copy(0, rows(trace_s, 0, 16), rows(halo_r, 0, 16), (flow - 1, col, row))),
            (flow < n_flow - 1, flow > 0, copy(1, rows(trace_s, 16, 16), rows(halo_r, 16, 16), (flow + 1, col, row))),
            (col > 0, col < n_col - 1, copy(2, rows(trace_s, 32, 8), rows(halo_r, 32, 8), (flow, col - 1, row))),
            (col < n_col - 1, col > 0, copy(3, rows(trace_s, 40, 8), rows(halo_r, 40, 8), (flow, col + 1, row))),
            (row > 0, row < n_row - 1, copy(4, zsend_s.at[s], z_r.at[s, 0], (flow, col, row - 1))),
            (row < n_row - 1, row > 0, copy(5, zsend_s.at[s], z_r.at[s, 1], (flow, col, row + 1))),
        )

    def forward(ref):
        fill = jnp.zeros((16 - ny, nz), F32)
        x = jnp.concatenate(
            [p for c in range(comps) for i in range(nx) for p in (ref[c, i], fill)], axis=0)
        x = jnp.concatenate([x, jnp.zeros((x.shape[0], BLK - nz), F32)], axis=1)
        y = bdot(left3(x), z_fwd)
        n = nx * 16
        return [bdot(a_fwd, right3(y[c * n : (c + 1) * n])) for c in range(comps)]

    def couple(parts, s, before_sends=None):
        pieces = [split(p) for p in parts]
        acc = None
        inner = []
        for c, (hi, lo) in enumerate(pieces):
            t = bdot(mxy, jnp.concatenate([hi, hi, lo], axis=0))
            trace_s[s, :, c * BLK : (c + 1) * BLK] = t[nh : nh + 48]
            inner.append(t[:nh])
        w = bdot(
            jnp.concatenate(
                [jnp.concatenate([p[h] for p in pieces], axis=0) for h in (0, 1, 0)], axis=1),
            kz)
        lanes = cols_of(128)
        for c in range(comps):
            wc = w[c * nh : (c + 1) * nh]
            keep = (lanes == nz - 128 + c) | (lanes == nz - 120 + c)
            piece = jnp.where(keep, wc[:, 128:256], 0.0)
            acc = piece if acc is None else acc + piece
            inner[c] = inner[c] + wc
        zsend_s[s] = acc
        if before_sends is not None:
            before_sends()
        for sends, _, copy in faces(s):
            pl.when(sends)(copy.start)
        return inner

    def finish(s):
        for _, receives, copy in faces(s):
            pl.when(receives)(copy.wait_recv)

    def update(parts, inner, s):
        zn, zp = z_r[s, 0], z_r[s, 1]
        r = r_s[...]
        new = []
        for c in range(comps):
            add = bdot(inj, right3(halo_r[s, :, c * BLK : (c + 1) * BLK]))
            zlo = zp[:, nz - 120 + c : nz - 119 + c] * zin0
            zhi = zn[:, nz - 128 + c : nz - 127 + c] * zin5
            total = inner[c] + add + jnp.concatenate([zlo, zhi], axis=1)
            new.append((1.0 - OMEGA) * parts[c] + r * (f_s[c] + TAU * total))
        return new

    local[1].wait()
    state = forward(u_in)
    inner = couple(
        state, 0, lambda: pl.semaphore_wait(barrier, (n_fc - 1) + (n_row - 1)))
    for c in range(comps):
        u_s[c] = state[c]

    local[2].wait()
    local[3].wait()
    pan_s[...] = jnp.zeros(pan_s.shape, F32)
    for n in range(NT - 1):
        pan_s[n * 4 : (n + 1) * 4, 0:pan] = hist_ref[n]
    pan_s[64:67, 0:pan] = pts_ref[...]
    narrow = pan_s[...]
    placed = narrow
    for i in range(1, n_row):
        placed = jnp.where(row == i, pltpu.roll(narrow, i * pan, 1), placed)
    pan_s[...] = placed
    for d in range(1, n_row):
        pan_copy(d).start()

    local[4].wait()
    for c, part in enumerate(forward(f_in)):
        f_s[c] = part
    for i in (5, 6, 7):
        local[i].wait()
    on_q = where01(rows_of(ez) == zqc).astype(BF16)
    lam2 = sum(bdot(p, on_q) for p in split(lam_ref[0]))
    den = lookup(vals_ref[0:1], ir) + lookup(vals_ref[1:2], jr) + lookup(vals_ref[2:3], zkc)
    for e in range(ey):
        den = den + where01(er == e) * lam2[e : e + 1]
    r_s[...] = jnp.where(inside, OMEGA / jnp.where(inside, den, 1.0), 0.0)

    a_back = pick(sx, nr, ic) * pick(sy, mjr, jc) * where01((mer == ec) & (myr < ny))
    a_back = left3(a_back)
    z_back = right3(pick(sz, zkr, zkc, True) * where01((zqr == zqc) & inside))
    zs = cols_of(128) - (row * pan).astype(F32)
    sq, sk = divmod_of(zs, N)
    z_new = pick(sz, zkr, sk, True) * where01((zqr == sq) & (zs >= 0) & (zs < pan))
    z_new = right3(z_new)
    own = where01(cols_of(n_obs) == rows_of(own_obs) + (row * own_obs).astype(F32))
    mine = ddot(own, obs_ref[...], NTD)
    half, freq = divmod_of(rows_of(2 * NF), NF)
    time, chan = divmod_of(cols_of(4 * NT), 4)
    sin_t, cos_t = sincos((freq + 0.5) * (math.pi / NF) * time)
    table = jnp.where(half == 0, cos_t, -sin_t)
    last = table[:, 4 * NT - 1 : 4 * NT]
    wide = jnp.concatenate([table * where01(chan == c) for c in range(4)], axis=0)

    finish(0)
    state = update([u_s[c] for c in range(comps)], inner, 0)
    inner = couple(state, 1)
    for c in range(comps):
        u_s[c] = state[c]

    for d in range(1, n_row):
        pan_copy(d).wait_recv()
    panels = pan_s[...]
    for d in range(1, n_row):
        panels = panels + pan_r[d]
    dx, dy, dz = (mine[:, a : a + 1] - panels[64 + a : 65 + a, :] for a in range(3))
    r2 = dx * dx + dy * dy + dz * dz
    radius = jnp.sqrt(r2)
    inv = 1.0 / radius
    dx, dy, dz = dx * inv, dy * inv, dz * inv
    amp = inv * (1.0 / (4.0 * math.pi))
    step = KMAX / NF
    sin_r, ar = sincos(radius * (0.5 * step))
    ai = -sin_r
    sr, si = ar * ar - ai * ai, 2.0 * ar * ai
    ar, ai = ar * amp, ai * amp
    spectral = ddot(wide, panels[0:64])
    lane128 = lax.broadcasted_iota(jnp.int32, (1, 128), 1)
    total = jnp.zeros((own_obs, 128), F32)
    for f in range(NF):
        k = step * (f + 0.5)
        er_s[f], ei_s[f] = ar, ai
        re = [spectral[2 * NF * c + f : 2 * NF * c + f + 1] for c in range(4)]
        im = [spectral[2 * NF * c + NF + f : 2 * NF * c + NF + f + 1] for c in range(4)]
        d_re = dx * re[1] + dy * re[2] + dz * re[3]
        d_im = dx * im[1] + dy * im[2] + dz * im[3]
        t_re = d_re * inv - k * (im[0] + d_im)
        t_im = d_im * inv + k * (re[0] + d_re)
        s_re = jnp.sum(ar * t_re - ai * t_im, axis=1, keepdims=True)
        s_im = jnp.sum(ar * t_im + ai * t_re, axis=1, keepdims=True)
        total = jnp.where(lane128 == f, s_re, total)
        total = jnp.where(lane128 == NF + f, s_im, total)
        if f < NF - 1:
            ar, ai = ar * sr - ai * si, ar * si + ai * sr

    finish(1)
    state = update([u_s[c] for c in range(comps)], inner, 1)
    pieces = [split(p) for p in state]
    corners = jnp.zeros((8, BLK), F32)
    for c in range(4):
        hi, lo = pieces[c]
        top = bdot(a_back[0:16], jnp.concatenate([hi, hi, lo], axis=0))[0:1]
        corners = jnp.where(t8 == c, top, corners)
    new_s[...] = bdot(left3(corners), z_new)
    for d in range(1, n_row):
        new_copy(d).start()

    w = bdot(
        jnp.concatenate(
            [jnp.concatenate([p[h] for p in pieces], axis=0) for h in (0, 1, 0)], axis=1),
        z_back)
    for c in range(comps):
        nodes = bdot(a_back, right3(w[c * nh : (c + 1) * nh]))
        for i in range(nx):
            out_buf[c, i] = nodes[i * 16 : i * 16 + ny, :nz]
    out_copy = pltpu.make_async_copy(out_buf, out_hbm, local_sem.at[8])
    out_copy.start()

    for d in range(1, n_row):
        new_copy(d).wait_recv()
    newest = new_s[...]
    for d in range(1, n_row):
        newest = newest + new_r[d]
    along = dx * newest[1:2] + dy * newest[2:3] + dz * newest[3:4]
    a_val = newest[0:1] + along
    b_val = along * inv
    fresh = jnp.zeros((own_obs, 128), F32)
    for f in range(NF):
        k = step * (f + 0.5)
        ka = k * a_val
        gr, gi = er_s[f], ei_s[f]
        s_re = jnp.sum(gr * b_val - gi * ka, axis=1, keepdims=True)
        s_im = jnp.sum(gr * ka + gi * b_val, axis=1, keepdims=True)
        fresh = jnp.where(lane128 == f, s_re, fresh)
        fresh = jnp.where(lane128 == NF + f, s_im, fresh)
    turned = jnp.concatenate([fresh, total], axis=0).T
    fr, fi = turned[0:NF], turned[NF : 2 * NF]
    c15, s15 = last[0:NF], last[NF : 2 * NF]
    part_re = c15 * fr - s15 * fi + pltpu.roll(fr, own_obs, 1)
    part_im = c15 * fi + s15 * fr + pltpu.roll(fi, own_obs, 1)
    part = jnp.where(lane128 < own_obs, part_re, pltpu.roll(part_im, own_obs, 1))
    part_s[...] = part
    part_r[fc] = part
    each_fc(lambda d: part_copy(d).start())
    each_fc(part_wait)
    if n_fc <= 16:
        spectra = part_r[0]
        for d in range(1, n_fc):
            spectra = spectra + part_r[d]
    else:
        spectra = lax.fori_loop(1, n_fc, lambda d, acc: acc + part_r[d], part_r[0])
    spec_ref[0] = spectra[:, :own_obs]
    spec_ref[1] = spectra[:, own_obs : 2 * own_obs]

    for s in range(SWEEPS):
        for sends, _, copy in faces(s):
            pl.when(sends)(copy.wait_send)
    for d in range(1, n_row):
        pan_copy(d).wait_send()
        new_copy(d).wait_send()
    each_fc(lambda d: part_copy(d).wait_send())
    out_copy.wait()


def on_device(forcing, previous, shift, bases, values, observers, points, history):
    n_flow, n_col, n_row = (lax.axis_size(a) for a in ("flow", "col", "row"))
    comps, nx, ny, nz = forcing.shape
    n_fc = n_flow * n_col
    pan = points.shape[1]
    n_obs = observers.shape[1]
    own_obs = n_obs // n_row
    nh = -(-nx * ny // 16) * 16
    sizes = (n_flow, n_col, n_row, comps, nx, ny, nz, pan, n_obs, nh)
    history = jnp.transpose(history, (1, 0, 2))
    vmem = pl.BlockSpec(memory_space=pltpu.VMEM)
    hbm = pl.BlockSpec(memory_space=pl.ANY)
    dma = pltpu.SemaphoreType.DMA
    return pl.pallas_call(
        functools.partial(kernel, sizes),
        out_shape=(
            jax.ShapeDtypeStruct(forcing.shape, F32),
            jax.ShapeDtypeStruct((2, NF, own_obs), F32),
        ),
        in_specs=[hbm] * 8,
        out_specs=(hbm, vmem),
        scratch_shapes=[
            pltpu.VMEM((comps, nx, ny, nz), F32),
            pltpu.VMEM((comps, nx, ny, nz), F32),
            pltpu.VMEM(shift.shape, F32),
            pltpu.VMEM(bases.shape, F32),
            pltpu.VMEM(values.shape, F32),
            pltpu.VMEM(observers.shape, F32),
            pltpu.VMEM(points.shape, F32),
            pltpu.VMEM(history.shape, F32),
            pltpu.VMEM((comps, nx, ny, nz), F32),
            pltpu.VMEM((comps, nh, BLK), F32),
            pltpu.VMEM((comps, nh, BLK), F32),
            pltpu.VMEM((nh, BLK), F32),
            pltpu.VMEM((SWEEPS, 48, comps * BLK), F32),
            pltpu.VMEM((SWEEPS, nh, 128), F32),
            pltpu.VMEM((SWEEPS, 48, comps * BLK), F32),
            pltpu.VMEM((SWEEPS, 2, nh, 128), F32),
            pltpu.VMEM((72, 128), F32),
            pltpu.VMEM((n_row, 72, 128), F32),
            pltpu.VMEM((8, 128), F32),
            pltpu.VMEM((n_row, 8, 128), F32),
            pltpu.VMEM((NF, own_obs, 128), F32),
            pltpu.VMEM((NF, own_obs, 128), F32),
            pltpu.VMEM((NF, 128), F32),
            pltpu.VMEM((n_fc, NF, 128), F32),
            dma((9,)),
            dma((SWEEPS, 6)),
            dma((SWEEPS, 6)),
            dma((n_row,)),
            dma((n_row,)),
            dma((n_row,)),
            dma((n_row,)),
            dma((n_fc,)),
            dma((n_fc,)),
        ],
        compiler_params=pltpu.CompilerParams(
            collective_id=0, has_side_effects=True, vmem_limit_bytes=60 * 1024 * 1024
        ),
    )(forcing, previous, shift, bases, values, observers, points, history)


def solution(mesh):
    return jax.shard_map(
        on_device,
        mesh=mesh,
        in_specs=(
            P(None, "flow", "col", "row"),
            P(None, "flow", "col", "row"),
            P("flow", "col", "row"),
            P(),
            P(),
            P(),
            P(None, ("flow", "col", "row")),
            P(None, None, ("flow", "col", "row")),
        ),
        out_specs=(P(None, "flow", "col", "row"), P(None, None, "row")),
        check_vma=False,
    )
```

```python
import functools
import math

import jax
import jax.numpy as jnp
from jax import lax
from jax.experimental import pallas as pl
from jax.experimental.pallas import tpu as pltpu
from jax.sharding import PartitionSpec as P

N = 6
SWEEPS = 2
NT = 16
NF = 16
OMEGA = 0.8
TAU = 0.5
KMAX = 2.0
BLK = 256
HIGH = lax.Precision.HIGHEST
MESH = pl.DeviceIdType.MESH
F32 = jnp.float32
BF16 = jnp.bfloat16
NN = (((1,), (0,)), ((), ()))
NTD = (((1,), (1,)), ((), ()))


def ddot(a, b, dims=NN):
    return lax.dot_general(a, b, dims, precision=HIGH, preferred_element_type=F32)


def bdot(a, b, dims=NN):
    return lax.dot_general(a, b, dims, preferred_element_type=F32)


def split(a):
    hi = a.astype(BF16)
    return hi, (a - hi.astype(F32)).astype(BF16)


def left3(a):
    hi, lo = split(a)
    return jnp.concatenate([hi, lo, hi], axis=1)


def right3(b):
    hi, lo = split(b)
    return jnp.concatenate([hi, hi, lo], axis=0)


def rows_of(n):
    return lax.broadcasted_iota(jnp.int32, (n, 1), 0).astype(F32)


def cols_of(n):
    return lax.broadcasted_iota(jnp.int32, (1, n), 1).astype(F32)


def divmod_of(v, n):
    q = jnp.floor((v + 0.5) * (1.0 / n))
    return q, v - n * q


def where01(cond):
    return jnp.where(cond, 1.0, 0.0).astype(F32)


def pick(m, r, c, transposed=False):
    on_r = where01(r == cols_of(N)).astype(BF16)
    on_c = where01(rows_of(N) == c).astype(BF16)
    total = None
    for part in split(m):
        left = bdot(on_r, part, NTD if transposed else NN).astype(BF16)
        out = bdot(left, on_c)
        total = out if total is None else total + out
    return total


def lookup(row, labels):
    total = None
    for k in range(N):
        term = row[:, k : k + 1] * where01(labels == k)
        total = term if total is None else total + term
    return total


def sincos(x):
    n = jnp.floor(x * (2.0 / math.pi) + 0.5)
    y = ((x - n * 1.5703125) - n * 4.83751296997e-4) - n * 7.54978995489e-8
    z = y * y
    s = y + y * z * (-1.6666654611e-1 + z * (8.3321608736e-3 - z * 1.9515295891e-4))
    c = 1.0 - 0.5 * z + z * z * (4.166664568298827e-2 - z * (1.388731625493765e-3 - z * 2.443315711809948e-5))
    q = n - 4.0 * jnp.floor(n * 0.25)
    odd = (q == 1.0) | (q == 3.0)
    sin = jnp.where(odd, c, s) * jnp.where(q >= 2.0, -1.0, 1.0)
    cos = jnp.where(odd, s, c) * jnp.where((q == 1.0) | (q == 2.0), -1.0, 1.0)
    return sin, cos


def kernel(
    sizes, f_hbm, u_hbm, lam_hbm, bases_hbm, vals_hbm, obs_hbm, pts_hbm, hist_hbm,
    out_hbm, spec_ref,
    f_in, u_in, lam_ref, bases_ref, vals_ref, obs_ref, pts_ref, hist_ref,
    out_buf, u_s, f_s, r_s, x_s, x_r, trace_s, zsend_s, halo_r, z_r,
    flat_s, pan_s, pan_r, new_s, new_r, er_s, ei_s, part_s, part_r,
    local_sem, hs_sem, hr_sem, ps_sem, pr_sem, ns_sem, nr_sem, ss_sem, sr_sem,
):
    n_flow, n_col, n_row, comps, nx, ny, nz, pan, n_obs, nh = sizes
    ey, ez = ny // N, nz // N
    own_obs = n_obs // n_row
    flow, col, row = (lax.axis_index(a) for a in ("flow", "col", "row"))
    n_fc = n_flow * n_col
    fc = flow * n_col + col

    def fc_peer(d):
        t = lax.rem(fc + d, n_fc)
        return (lax.div(t, n_col), lax.rem(t, n_col), row)

    def row_peer(d):
        return (flow, col, lax.rem(row + d, n_row))

    def each_fc(body):
        if n_fc <= 16:
            for d in range(1, n_fc):
                body(d)
        else:
            lax.fori_loop(1, n_fc, lambda d, c: (body(d), c)[1], 0)

    pairs = (
        (bases_hbm, bases_ref), (u_hbm, u_in), (pts_hbm, pts_ref), (hist_hbm, hist_ref),
        (f_hbm, f_in), (lam_hbm, lam_ref), (vals_hbm, vals_ref), (obs_hbm, obs_ref),
    )
    local = [pltpu.make_async_copy(a, b, local_sem.at[i]) for i, (a, b) in enumerate(pairs)]
    for copy in local:
        copy.start()
    halo_r[...] = jnp.zeros(halo_r.shape, F32)
    x_r[...] = jnp.zeros(x_r.shape, F32)
    z_r[...] = jnp.zeros(z_r.shape, F32)
    barrier = pltpu.get_barrier_semaphore()
    each_fc(lambda d: pl.semaphore_signal(barrier, inc=1, device_id=fc_peer(d), device_id_type=MESH))
    for d in range(1, n_row):
        pl.semaphore_signal(barrier, inc=1, device_id=row_peer(d), device_id_type=MESH)

    local[0].wait()
    sx, sy, sz = bases_ref[0], bases_ref[1], bases_ref[2]

    def ends(m, labels):
        return lookup(m[0:1], labels), lookup(m[N - 1 : N], labels)

    hr = rows_of(nh)
    hc = cols_of(nh)
    ir, yr = divmod_of(hr, ny)
    er, jr = divmod_of(yr, N)
    ic, yc = divmod_of(hc, ny)
    ec, jc = divmod_of(yc, N)
    x0r, x5r = ends(sx, ic)
    y0r, y5r = ends(sy, jc)
    x0c, x5c = ends(sx, ir)
    y0c, y5c = ends(sy, jr)

    nc, myc = divmod_of(cols_of(nx * 16), 16)
    mec, mjc = divmod_of(myc, N)
    nr, myr = divmod_of(rows_of(nx * 16), 16)
    mer, mjr = divmod_of(myr, N)
    a_fwd = pick(sx, ir, nc, True) * pick(sy, jr, mjc, True) * where01((er == mec) & (myc < ny))
    lane = cols_of(BLK)
    inside = lane < nz
    zqr, zkr = divmod_of(rows_of(BLK), N)
    zqc, zkc = divmod_of(lane, N)
    z_fwd = pick(sz, zkr, zkc) * where01((zqr == zqc) & inside)
    a_fwd = left3(a_fwd)
    z_fwd = right3(z_fwd)

    z0r, z5r = ends(sz, zkc)
    z0c, z5c = ends(sz, zkr)
    kz = where01((zqr == zqc + 1) & inside & (zqr < ez)) * z0c * z5r
    kz = kz + where01((zqr == zqc - 1) & inside) * z5c * z0r
    first_lane = (lane >= nz) & (lane < nz + comps)
    last_lane = (lane >= nz + 8) & (lane < nz + 8 + comps)
    kz = kz + where01((zqr == 0) & first_lane) * z0c + where01((zqr == ez - 1) & last_lane) * z5c
    kz = right3(kz)

    ky = where01(ir == ic) * (
        where01(ec == er + 1) * y5c * y0r + where01(ec == er - 1) * y0c * y5r
    )
    t16, t8 = rows_of(16), rows_of(8)
    mxy = jnp.concatenate(
        [
            ky,
            where01(t16 == yc) * x0r,
            where01(t16 == yc) * x5r,
            where01((t8 == ic) & (ec == 0)) * y0r,
            where01((t8 == ic) & (ec == ey - 1)) * y5r,
        ],
        axis=0,
    )
    mxy = left3(mxy)
    hl = cols_of(48)
    inj = where01(hl == yr) * x5c + where01(hl == yr + 16) * x0c
    inj = inj + where01((hl == ir + 32) & (er == ey - 1)) * y5c
    inj = inj + where01((hl == ir + 40) & (er == 0)) * y0c
    inj = left3(inj)
    zin5 = jnp.where(zqc == ez - 1, z5r, 0.0)[:, 128:256]
    zin0 = jnp.where(zqc == 0, z0r, 0.0)[:, 0:128]

    def pan_copy(d):
        return pltpu.make_async_remote_copy(
            src_ref=pan_s, dst_ref=pan_r.at[row], send_sem=ps_sem.at[d], recv_sem=pr_sem.at[d],
            device_id=row_peer(d), device_id_type=MESH)

    def pan_wait(d):
        src = lax.rem(row + (n_row - d), n_row)
        pltpu.make_async_remote_copy(
            src_ref=pan_s, dst_ref=pan_r.at[src], send_sem=ps_sem.at[d], recv_sem=pr_sem.at[d],
            device_id=row_peer(d), device_id_type=MESH).wait_recv()

    def new_copy(d):
        return pltpu.make_async_remote_copy(
            src_ref=new_s, dst_ref=new_r.at[d], send_sem=ns_sem.at[d], recv_sem=nr_sem.at[d],
            device_id=row_peer(d), device_id_type=MESH)

    def part_copy(d):
        return pltpu.make_async_remote_copy(
            src_ref=part_s, dst_ref=part_r.at[fc], send_sem=ss_sem.at[d], recv_sem=sr_sem.at[d],
            device_id=fc_peer(d), device_id_type=MESH)

    def part_wait(d):
        src = lax.rem(fc + (n_fc - d), n_fc)
        pltpu.make_async_remote_copy(
            src_ref=part_s, dst_ref=part_r.at[src], send_sem=ss_sem.at[d], recv_sem=sr_sem.at[d],
            device_id=fc_peer(d), device_id_type=MESH).wait_recv()

    def faces(s):
        def copy(k, src, dst, where):
            return pltpu.make_async_remote_copy(
                src_ref=src, dst_ref=dst, send_sem=hs_sem.at[s, k], recv_sem=hr_sem.at[s, k],
                device_id=where, device_id_type=MESH)

        def rows(buf, a, n):
            return buf.at[s, pl.ds(a, n), :]

        return (
            (flow > 0, flow < n_flow - 1, copy(0, x_s.at[s, 0], x_r.at[s, 0], (flow - 1, col, row))),
            (flow < n_flow - 1, flow > 0, copy(1, x_s.at[s, 1], x_r.at[s, 1], (flow + 1, col, row))),
            (col > 0, col < n_col - 1, copy(2, rows(trace_s, 0, 8), rows(halo_r, 0, 8), (flow, col - 1, row))),
            (col < n_col - 1, col > 0, copy(3, rows(trace_s, 8, 8), rows(halo_r, 8, 8), (flow, col + 1, row))),
            (row > 0, row < n_row - 1, copy(4, zsend_s.at[s], z_r.at[s, 0], (flow, col, row - 1))),
            (row < n_row - 1, row > 0, copy(5, zsend_s.at[s], z_r.at[s, 1], (flow, col, row + 1))),
        )

    def forward(ref):
        fill = jnp.zeros((16 - ny, nz), F32)
        x = jnp.concatenate(
            [p for c in range(comps) for i in range(nx) for p in (ref[c, i], fill)], axis=0)
        x = jnp.concatenate([x, jnp.zeros((x.shape[0], BLK - nz), F32)], axis=1)
        y = bdot(left3(x), z_fwd)
        n = nx * 16
        return [bdot(a_fwd, right3(y[c * n : (c + 1) * n])) for c in range(comps)]

    tiles = 2 * -(-(comps + (comps + 1) // 2) // 2)
    half_tiles = tiles // 2

    def pack_x(faces_of, s, side):
        lows = [t[:, :128] for t in faces_of]
        highs = [t[:, 128:] for t in faces_of]
        both = lows + [
            highs[i] + pltpu.roll(highs[i + 1], 64, 1) if i + 1 < comps else highs[i]
            for i in range(0, comps, 2)
        ]
        both = both + [jnp.zeros((16, 128), F32)] * (tiles - len(both))
        for a in range(tiles):
            x_s[s, side, :, a * 128 : (a + 1) * 128] = both[a][0:8]
        for a in range(half_tiles):
            b = tiles + a
            x_s[s, side, :, b * 128 : (b + 1) * 128] = both[a][8:16] + pltpu.roll(
                both[a + half_tiles][8:16], 4, 0)

    def unpack_x(s, side):
        def tile(a):
            return x_r[s, side, :, a * 128 : (a + 1) * 128]

        both = []
        for a in range(tiles):
            rest = tile(tiles + a % half_tiles)
            if a >= half_tiles:
                rest = pltpu.roll(rest, 4, 0)
            both.append(jnp.concatenate([tile(a), rest], axis=0))
        faces_of = []
        for c in range(comps):
            high = both[comps + c // 2]
            if c % 2:
                high = pltpu.roll(high, 64, 1)
            faces_of.append(jnp.concatenate([both[c], high], axis=1))
        return faces_of

    def couple(parts, s, before_sends=None):
        pieces = [split(p) for p in parts]
        acc = None
        inner = []
        x_faces = []
        for c, (hi, lo) in enumerate(pieces):
            t = bdot(mxy, jnp.concatenate([hi, hi, lo], axis=0))
            trace_s[s, :, c * BLK : (c + 1) * BLK] = t[nh + 32 : nh + 48]
            x_faces.append(t[nh : nh + 32])
            inner.append(t[:nh])
        pack_x([t[:16] for t in x_faces], s, 0)
        pack_x([t[16:] for t in x_faces], s, 1)
        w = bdot(
            jnp.concatenate(
                [jnp.concatenate([p[h] for p in pieces], axis=0) for h in (0, 1, 0)], axis=1),
            kz)
        lanes = cols_of(128)
        for c in range(comps):
            wc = w[c * nh : (c + 1) * nh]
            keep = (lanes == nz - 128 + c) | (lanes == nz - 120 + c)
            piece = jnp.where(keep, wc[:, 128:256], 0.0)
            acc = piece if acc is None else acc + piece
            inner[c] = inner[c] + wc
        zsend_s[s] = acc
        if before_sends is not None:
            before_sends()
        for sends, _, copy in faces(s):
            pl.when(sends)(copy.start)
        return inner

    def finish(s):
        for _, receives, copy in faces(s):
            pl.when(receives)(copy.wait_recv)

    def update(parts, inner, s):
        zn, zp = z_r[s, 0], z_r[s, 1]
        r = r_s[...]
        new = []
        below, above = unpack_x(s, 0), unpack_x(s, 1)
        for c in range(comps):
            sides = [below[c], above[c], halo_r[s, :, c * BLK : (c + 1) * BLK]]
            add = bdot(inj, right3(jnp.concatenate(sides, axis=0)))
            zlo = zp[:, nz - 120 + c : nz - 119 + c] * zin0
            zhi = zn[:, nz - 128 + c : nz - 127 + c] * zin5
            total = inner[c] + add + jnp.concatenate([zlo, zhi], axis=1)
            new.append((1.0 - OMEGA) * parts[c] + r * (f_s[c] + TAU * total))
        return new

    local[1].wait()
    state = forward(u_in)
    inner = couple(
        state, 0, lambda: pl.semaphore_wait(barrier, (n_fc - 1) + (n_row - 1)))
    for c in range(comps):
        u_s[c] = state[c]

    local[2].wait()
    local[3].wait()
    flat_s[...] = jnp.zeros(flat_s.shape, F32)
    for n in range(NT - 1):
        flat_s[n * 4 : (n + 1) * 4, 0:pan] = hist_ref[n]
    flat_s[64:67, 0:pan] = pts_ref[...]
    packed = flat_s[0:24]
    for g in (1, 2):
        packed = packed + pltpu.roll(flat_s[g * 24 : (g + 1) * 24], g * pan, 1)
    pan_s[...] = packed
    pan_r[row] = packed
    for d in range(1, n_row):
        pan_copy(d).start()

    local[4].wait()
    for c, part in enumerate(forward(f_in)):
        f_s[c] = part
    for i in (5, 6, 7):
        local[i].wait()
    on_q = where01(rows_of(ez) == zqc).astype(BF16)
    lam2 = sum(bdot(p, on_q) for p in split(lam_ref[0]))
    den = lookup(vals_ref[0:1], ir) + lookup(vals_ref[1:2], jr) + lookup(vals_ref[2:3], zkc)
    for e in range(ey):
        den = den + where01(er == e) * lam2[e : e + 1]
    r_s[...] = jnp.where(inside, OMEGA / jnp.where(inside, den, 1.0), 0.0)

    a_back = pick(sx, nr, ic) * pick(sy, mjr, jc) * where01((mer == ec) & (myr < ny))
    a_back = left3(a_back)
    z_back = right3(pick(sz, zkr, zkc, True) * where01((zqr == zqc) & inside))
    zs = cols_of(128) - (row * pan).astype(F32)
    sq, sk = divmod_of(zs, N)
    z_new = pick(sz, zkr, sk, True) * where01((zqr == sq) & (zs >= 0) & (zs < pan))
    z_new = right3(z_new)
    own = where01(cols_of(n_obs) == rows_of(own_obs) + (row * own_obs).astype(F32))
    mine = ddot(own, obs_ref[...], NTD)
    half, freq = divmod_of(rows_of(2 * NF), NF)
    time, chan = divmod_of(cols_of(4 * NT), 4)
    sin_t, cos_t = sincos((freq + 0.5) * (math.pi / NF) * time)
    table = jnp.where(half == 0, cos_t, -sin_t)
    last = table[:, 4 * NT - 1 : 4 * NT]
    wide = jnp.concatenate([table * where01(chan == c) for c in range(4)], axis=0)

    finish(0)
    state = update([u_s[c] for c in range(comps)], inner, 0)
    inner = couple(state, 1)
    for c in range(comps):
        u_s[c] = state[c]

    for d in range(1, n_row):
        pan_wait(d)
    groups = []
    for g in range(3):
        group = jnp.zeros((24, 128), F32)
        for i in range(n_row):
            shift = ((i - g) * pan) % 128
            moved = pan_r[i] if shift == 0 else pltpu.roll(pan_r[i], shift, 1)
            here = (cols_of(128) >= i * pan) & (cols_of(128) < (i + 1) * pan)
            group = jnp.where(here, moved, group)
        groups.append(group)
    panels = jnp.concatenate(groups, axis=0)
    dx, dy, dz = (mine[:, a : a + 1] - panels[64 + a : 65 + a, :] for a in range(3))
    r2 = dx * dx + dy * dy + dz * dz
    radius = jnp.sqrt(r2)
    inv = 1.0 / radius
    dx, dy, dz = dx * inv, dy * inv, dz * inv
    amp = inv * (1.0 / (4.0 * math.pi))
    step = KMAX / NF
    sin_r, ar = sincos(radius * (0.5 * step))
    ai = -sin_r
    sr, si = ar * ar - ai * ai, 2.0 * ar * ai
    ar, ai = ar * amp, ai * amp
    spectral = ddot(wide, panels[0:64])
    lane128 = lax.broadcasted_iota(jnp.int32, (1, 128), 1)
    total = jnp.zeros((own_obs, 128), F32)
    for f in range(NF):
        k = step * (f + 0.5)
        er_s[f], ei_s[f] = ar, ai
        re = [spectral[2 * NF * c + f : 2 * NF * c + f + 1] for c in range(4)]
        im = [spectral[2 * NF * c + NF + f : 2 * NF * c + NF + f + 1] for c in range(4)]
        d_re = dx * re[1] + dy * re[2] + dz * re[3]
        d_im = dx * im[1] + dy * im[2] + dz * im[3]
        t_re = d_re * inv - k * (im[0] + d_im)
        t_im = d_im * inv + k * (re[0] + d_re)
        s_re = jnp.sum(ar * t_re - ai * t_im, axis=1, keepdims=True)
        s_im = jnp.sum(ar * t_im + ai * t_re, axis=1, keepdims=True)
        total = jnp.where(lane128 == f, s_re, total)
        total = jnp.where(lane128 == NF + f, s_im, total)
        if f < NF - 1:
            ar, ai = ar * sr - ai * si, ar * si + ai * sr

    finish(1)
    state = update([u_s[c] for c in range(comps)], inner, 1)
    pieces = [split(p) for p in state]
    corners = jnp.zeros((8, BLK), F32)
    for c in range(4):
        hi, lo = pieces[c]
        top = bdot(a_back[0:16], jnp.concatenate([hi, hi, lo], axis=0))[0:1]
        corners = jnp.where(t8 == c, top, corners)
    new_s[...] = bdot(left3(corners), z_new)
    for d in range(1, n_row):
        new_copy(d).start()

    w = bdot(
        jnp.concatenate(
            [jnp.concatenate([p[h] for p in pieces], axis=0) for h in (0, 1, 0)], axis=1),
        z_back)
    for c in range(comps):
        nodes = bdot(a_back, right3(w[c * nh : (c + 1) * nh]))
        for i in range(nx):
            out_buf[c, i] = nodes[i * 16 : i * 16 + ny, :nz]
    out_copy = pltpu.make_async_copy(out_buf, out_hbm, local_sem.at[8])
    out_copy.start()

    for d in range(1, n_row):
        new_copy(d).wait_recv()
    newest = new_s[...]
    for d in range(1, n_row):
        newest = newest + new_r[d]
    along = dx * newest[1:2] + dy * newest[2:3] + dz * newest[3:4]
    a_val = newest[0:1] + along
    b_val = along * inv
    fresh = jnp.zeros((own_obs, 128), F32)
    for f in range(NF):
        k = step * (f + 0.5)
        ka = k * a_val
        gr, gi = er_s[f], ei_s[f]
        s_re = jnp.sum(gr * b_val - gi * ka, axis=1, keepdims=True)
        s_im = jnp.sum(gr * ka + gi * b_val, axis=1, keepdims=True)
        fresh = jnp.where(lane128 == f, s_re, fresh)
        fresh = jnp.where(lane128 == NF + f, s_im, fresh)
    turned = jnp.concatenate([fresh, total], axis=0).T
    fr, fi = turned[0:NF], turned[NF : 2 * NF]
    c15, s15 = last[0:NF], last[NF : 2 * NF]
    part_re = c15 * fr - s15 * fi + pltpu.roll(fr, own_obs, 1)
    part_im = c15 * fi + s15 * fr + pltpu.roll(fi, own_obs, 1)
    part = jnp.where(lane128 < own_obs, part_re, pltpu.roll(part_im, own_obs, 1))
    part_s[...] = part
    part_r[fc] = part
    each_fc(lambda d: part_copy(d).start())
    each_fc(part_wait)
    if n_fc <= 16:
        spectra = part_r[0]
        for d in range(1, n_fc):
            spectra = spectra + part_r[d]
    else:
        spectra = lax.fori_loop(1, n_fc, lambda d, acc: acc + part_r[d], part_r[0])
    spec_ref[0] = spectra[:, :own_obs]
    spec_ref[1] = spectra[:, own_obs : 2 * own_obs]

    for s in range(SWEEPS):
        for sends, _, copy in faces(s):
            pl.when(sends)(copy.wait_send)
    for d in range(1, n_row):
        pan_copy(d).wait_send()
        new_copy(d).wait_send()
    each_fc(lambda d: part_copy(d).wait_send())
    out_copy.wait()


def on_device(forcing, previous, shift, bases, values, observers, points, history):
    n_flow, n_col, n_row = (lax.axis_size(a) for a in ("flow", "col", "row"))
    comps, nx, ny, nz = forcing.shape
    n_fc = n_flow * n_col
    pan = points.shape[1]
    n_obs = observers.shape[1]
    own_obs = n_obs // n_row
    nh = -(-nx * ny // 16) * 16
    sizes = (n_flow, n_col, n_row, comps, nx, ny, nz, pan, n_obs, nh)
    tiles = 2 * -(-(comps + (comps + 1) // 2) // 2)
    history = jnp.transpose(history, (1, 0, 2))
    vmem = pl.BlockSpec(memory_space=pltpu.VMEM)
    hbm = pl.BlockSpec(memory_space=pl.ANY)
    dma = pltpu.SemaphoreType.DMA
    return pl.pallas_call(
        functools.partial(kernel, sizes),
        out_shape=(
            jax.ShapeDtypeStruct(forcing.shape, F32),
            jax.ShapeDtypeStruct((2, NF, own_obs), F32),
        ),
        in_specs=[pl.BlockSpec(memory_space=pltpu.HBM)] * 8,
        out_specs=(hbm, vmem),
        scratch_shapes=[
            pltpu.VMEM((comps, nx, ny, nz), F32),
            pltpu.VMEM((comps, nx, ny, nz), F32),
            pltpu.VMEM(shift.shape, F32),
            pltpu.VMEM(bases.shape, F32),
            pltpu.VMEM(values.shape, F32),
            pltpu.VMEM(observers.shape, F32),
            pltpu.VMEM(points.shape, F32),
            pltpu.VMEM(history.shape, F32),
            pltpu.VMEM((comps, nx, ny, nz), F32),
            pltpu.VMEM((comps, nh, BLK), F32),
            pltpu.VMEM((comps, nh, BLK), F32),
            pltpu.VMEM((nh, BLK), F32),
            pltpu.VMEM((SWEEPS, 2, 8, tiles * 192), F32),
            pltpu.VMEM((SWEEPS, 2, 8, tiles * 192), F32),
            pltpu.VMEM((SWEEPS, 16, comps * BLK), F32),
            pltpu.VMEM((SWEEPS, nh, 128), F32),
            pltpu.VMEM((SWEEPS, 16, comps * BLK), F32),
            pltpu.VMEM((SWEEPS, 2, nh, 128), F32),
            pltpu.VMEM((72, 128), F32),
            pltpu.VMEM((24, 128), F32),
            pltpu.VMEM((n_row, 24, 128), F32),
            pltpu.VMEM((8, 128), F32),
            pltpu.VMEM((n_row, 8, 128), F32),
            pltpu.VMEM((NF, own_obs, 128), F32),
            pltpu.VMEM((NF, own_obs, 128), F32),
            pltpu.VMEM((NF, 128), F32),
            pltpu.VMEM((n_fc, NF, 128), F32),
            dma((9,)),
            dma((SWEEPS, 6)),
            dma((SWEEPS, 6)),
            dma((n_row,)),
            dma((n_row,)),
            dma((n_row,)),
            dma((n_row,)),
            dma((n_fc,)),
            dma((n_fc,)),
        ],
        compiler_params=pltpu.CompilerParams(
            collective_id=0, has_side_effects=True, vmem_limit_bytes=60 * 1024 * 1024
        ),
    )(forcing, previous, shift, bases, values, observers, points, history)


def solution(mesh):
    return jax.shard_map(
        on_device,
        mesh=mesh,
        in_specs=(
            P(None, "flow", "col", "row"),
            P(None, "flow", "col", "row"),
            P("flow", "col", "row"),
            P(),
            P(),
            P(),
            P(None, ("flow", "col", "row")),
            P(None, None, ("flow", "col", "row")),
        ),
        out_specs=(P(None, "flow", "col", "row"), P(None, None, "row")),
        check_vma=False,
    )
```

```python
import functools
import math

import jax
import jax.numpy as jnp
from jax import lax
from jax.experimental import pallas as pl
from jax.experimental.pallas import tpu as pltpu
from jax.sharding import PartitionSpec as P

N = 6
SWEEPS = 2
NT = 16
NF = 16
OMEGA = 0.8
TAU = 0.5
KMAX = 2.0
BLK = 256
HIGH = lax.Precision.HIGHEST
MESH = pl.DeviceIdType.MESH
F32 = jnp.float32
BF16 = jnp.bfloat16
NN = (((1,), (0,)), ((), ()))
NTD = (((1,), (1,)), ((), ()))


def ddot(a, b, dims=NN):
    return lax.dot_general(a, b, dims, precision=HIGH, preferred_element_type=F32)


def bdot(a, b, dims=NN):
    return lax.dot_general(a, b, dims, preferred_element_type=F32)


def split(a):
    hi = a.astype(BF16)
    return hi, (a - hi.astype(F32)).astype(BF16)


def left3(a):
    hi, lo = split(a)
    return jnp.concatenate([hi, lo, hi], axis=1)


def right3(b):
    hi, lo = split(b)
    return jnp.concatenate([hi, hi, lo], axis=0)


def rows_of(n):
    return lax.broadcasted_iota(jnp.int32, (n, 1), 0).astype(F32)


def cols_of(n):
    return lax.broadcasted_iota(jnp.int32, (1, n), 1).astype(F32)


def divmod_of(v, n):
    q = jnp.floor((v + 0.5) * (1.0 / n))
    return q, v - n * q


def where01(cond):
    return jnp.where(cond, 1.0, 0.0).astype(F32)


def pick(m, r, c, transposed=False):
    on_r = where01(r == cols_of(N)).astype(BF16)
    on_c = where01(rows_of(N) == c).astype(BF16)
    total = None
    for part in split(m):
        left = bdot(on_r, part, NTD if transposed else NN).astype(BF16)
        out = bdot(left, on_c)
        total = out if total is None else total + out
    return total


def lookup(row, labels):
    total = None
    for k in range(N):
        term = row[:, k : k + 1] * where01(labels == k)
        total = term if total is None else total + term
    return total


def sincos(x):
    n = jnp.floor(x * (2.0 / math.pi) + 0.5)
    y = ((x - n * 1.5703125) - n * 4.83751296997e-4) - n * 7.54978995489e-8
    z = y * y
    s = y + y * z * (-1.6666654611e-1 + z * (8.3321608736e-3 - z * 1.9515295891e-4))
    c = 1.0 - 0.5 * z + z * z * (4.166664568298827e-2 - z * (1.388731625493765e-3 - z * 2.443315711809948e-5))
    q = n - 4.0 * jnp.floor(n * 0.25)
    odd = (q == 1.0) | (q == 3.0)
    sin = jnp.where(odd, c, s) * jnp.where(q >= 2.0, -1.0, 1.0)
    cos = jnp.where(odd, s, c) * jnp.where((q == 1.0) | (q == 2.0), -1.0, 1.0)
    return sin, cos


def kernel(
    sizes, f_hbm, u_hbm, lam_hbm, bases_hbm, vals_hbm, obs_hbm, pts_hbm, hist_hbm,
    out_hbm, spec_ref,
    f_in, u_in, lam_ref, bases_ref, vals_ref, obs_ref, pts_ref, hist_ref,
    out_buf, u_s, f_s, r_s, x_s, x_r, trace_s, zsend_s, halo_r, z_r,
    flat_s, pan_s, pan_r, new_s, new_r, er_s, ei_s, part_s, part_r,
    local_sem, hs_sem, hr_sem, ps_sem, pr_sem, ns_sem, nr_sem, ss_sem, sr_sem,
):
    n_flow, n_col, n_row, comps, nx, ny, nz, pan, n_obs, nh = sizes
    ey, ez = ny // N, nz // N
    own_obs = n_obs // n_row
    flow, col, row = (lax.axis_index(a) for a in ("flow", "col", "row"))
    n_fc = n_flow * n_col
    fc = flow * n_col + col

    def fc_peer(d):
        t = lax.rem(fc + d, n_fc)
        return (lax.div(t, n_col), lax.rem(t, n_col), row)

    def row_peer(d):
        return (flow, col, lax.rem(row + d, n_row))

    def each_fc(body):
        if n_fc <= 16:
            for d in range(1, n_fc):
                body(d)
        else:
            lax.fori_loop(1, n_fc, lambda d, c: (body(d), c)[1], 0)

    pairs = (
        (bases_hbm, bases_ref), (u_hbm, u_in), (pts_hbm, pts_ref), (hist_hbm, hist_ref),
        (f_hbm, f_in), (lam_hbm, lam_ref), (vals_hbm, vals_ref), (obs_hbm, obs_ref),
    )
    local = [pltpu.make_async_copy(a, b, local_sem.at[i]) for i, (a, b) in enumerate(pairs)]
    for copy in local:
        copy.start()
    halo_r[...] = jnp.zeros(halo_r.shape, F32)
    x_r[...] = jnp.zeros(x_r.shape, F32)
    z_r[...] = jnp.zeros(z_r.shape, F32)
    barrier = pltpu.get_barrier_semaphore()
    each_fc(lambda d: pl.semaphore_signal(barrier, inc=1, device_id=fc_peer(d), device_id_type=MESH))
    for d in range(1, n_row):
        pl.semaphore_signal(barrier, inc=1, device_id=row_peer(d), device_id_type=MESH)

    local[0].wait()
    sx, sy, sz = bases_ref[0], bases_ref[1], bases_ref[2]

    def ends(m, labels):
        return lookup(m[0:1], labels), lookup(m[N - 1 : N], labels)

    hr = rows_of(nh)
    hc = cols_of(nh)
    ir, yr = divmod_of(hr, ny)
    er, jr = divmod_of(yr, N)
    ic, yc = divmod_of(hc, ny)
    ec, jc = divmod_of(yc, N)
    x0r, x5r = ends(sx, ic)
    y0r, y5r = ends(sy, jc)
    x0c, x5c = ends(sx, ir)
    y0c, y5c = ends(sy, jr)

    nc, myc = divmod_of(cols_of(nx * 16), 16)
    mec, mjc = divmod_of(myc, N)
    nr, myr = divmod_of(rows_of(nx * 16), 16)
    mer, mjr = divmod_of(myr, N)
    a_fwd = pick(sx, ir, nc, True) * pick(sy, jr, mjc, True) * where01((er == mec) & (myc < ny))
    lane = cols_of(BLK)
    inside = lane < nz
    zqr, zkr = divmod_of(rows_of(BLK), N)
    zqc, zkc = divmod_of(lane, N)
    z_fwd = pick(sz, zkr, zkc) * where01((zqr == zqc) & inside)
    a_fwd = left3(a_fwd)
    z_fwd = right3(z_fwd)

    z0r, z5r = ends(sz, zkc)
    z0c, z5c = ends(sz, zkr)
    kz = where01((zqr == zqc + 1) & inside & (zqr < ez)) * z0c * z5r
    kz = kz + where01((zqr == zqc - 1) & inside) * z5c * z0r
    first_lane = (lane >= nz) & (lane < nz + comps)
    last_lane = (lane >= nz + 8) & (lane < nz + 8 + comps)
    kz = kz + where01((zqr == 0) & first_lane) * z0c + where01((zqr == ez - 1) & last_lane) * z5c
    kz = right3(kz)

    ky = where01(ir == ic) * (
        where01(ec == er + 1) * y5c * y0r + where01(ec == er - 1) * y0c * y5r
    )
    t16, t8 = rows_of(16), rows_of(8)
    mxy = jnp.concatenate(
        [
            ky,
            where01(t16 == yc) * x0r,
            where01(t16 == yc) * x5r,
            where01((t8 == ic) & (ec == 0)) * y0r,
            where01((t8 == ic) & (ec == ey - 1)) * y5r,
        ],
        axis=0,
    )
    mxy = left3(mxy)
    hl = cols_of(48)
    inj = where01(hl == yr) * x5c + where01(hl == yr + 16) * x0c
    inj = inj + where01((hl == ir + 32) & (er == ey - 1)) * y5c
    inj = inj + where01((hl == ir + 40) & (er == 0)) * y0c
    inj = left3(inj)
    zin5 = jnp.where(zqc == ez - 1, z5r, 0.0)[:, 128:256]
    zin0 = jnp.where(zqc == 0, z0r, 0.0)[:, 0:128]

    def pan_copy(d):
        return pltpu.make_async_remote_copy(
            src_ref=pan_s, dst_ref=pan_r.at[row], send_sem=ps_sem.at[d], recv_sem=pr_sem.at[d],
            device_id=row_peer(d), device_id_type=MESH)

    def pan_wait(d):
        src = lax.rem(row + (n_row - d), n_row)
        pltpu.make_async_remote_copy(
            src_ref=pan_s, dst_ref=pan_r.at[src], send_sem=ps_sem.at[d], recv_sem=pr_sem.at[d],
            device_id=row_peer(d), device_id_type=MESH).wait_recv()

    def new_copy(d):
        return pltpu.make_async_remote_copy(
            src_ref=new_s, dst_ref=new_r.at[d], send_sem=ns_sem.at[d], recv_sem=nr_sem.at[d],
            device_id=row_peer(d), device_id_type=MESH)

    def part_copy(d):
        return pltpu.make_async_remote_copy(
            src_ref=part_s, dst_ref=part_r.at[fc], send_sem=ss_sem.at[d], recv_sem=sr_sem.at[d],
            device_id=fc_peer(d), device_id_type=MESH)

    def part_wait(d):
        src = lax.rem(fc + (n_fc - d), n_fc)
        pltpu.make_async_remote_copy(
            src_ref=part_s, dst_ref=part_r.at[src], send_sem=ss_sem.at[d], recv_sem=sr_sem.at[d],
            device_id=fc_peer(d), device_id_type=MESH).wait_recv()

    def faces(s):
        def copy(k, src, dst, where):
            return pltpu.make_async_remote_copy(
                src_ref=src, dst_ref=dst, send_sem=hs_sem.at[s, k], recv_sem=hr_sem.at[s, k],
                device_id=where, device_id_type=MESH)

        def rows(buf, a, n):
            return buf.at[s, pl.ds(a, n), :]

        return (
            (flow > 0, flow < n_flow - 1, copy(0, x_s.at[s, 0], x_r.at[s, 0], (flow - 1, col, row))),
            (flow < n_flow - 1, flow > 0, copy(1, x_s.at[s, 1], x_r.at[s, 1], (flow + 1, col, row))),
            (col > 0, col < n_col - 1, copy(2, rows(trace_s, 0, 8), rows(halo_r, 0, 8), (flow, col - 1, row))),
            (col < n_col - 1, col > 0, copy(3, rows(trace_s, 8, 8), rows(halo_r, 8, 8), (flow, col + 1, row))),
            (row > 0, row < n_row - 1, copy(4, zsend_s.at[s], z_r.at[s, 0], (flow, col, row - 1))),
            (row < n_row - 1, row > 0, copy(5, zsend_s.at[s], z_r.at[s, 1], (flow, col, row + 1))),
        )

    def forward(ref):
        fill = jnp.zeros((16 - ny, nz), F32)
        x = jnp.concatenate(
            [p for c in range(comps) for i in range(nx) for p in (ref[c, i], fill)], axis=0)
        x = jnp.concatenate([x, jnp.zeros((x.shape[0], BLK - nz), F32)], axis=1)
        y = bdot(left3(x), z_fwd)
        n = nx * 16
        return [bdot(a_fwd, right3(y[c * n : (c + 1) * n])) for c in range(comps)]

    tiles = 2 * -(-(comps + (comps + 1) // 2) // 2)
    half_tiles = tiles // 2

    def pack_x(faces_of, s, side):
        lows = [t[:, :128] for t in faces_of]
        highs = [t[:, 128:] for t in faces_of]
        both = lows + [
            highs[i] + pltpu.roll(highs[i + 1], 64, 1) if i + 1 < comps else highs[i]
            for i in range(0, comps, 2)
        ]
        both = both + [jnp.zeros((16, 128), F32)] * (tiles - len(both))
        for a in range(tiles):
            x_s[s, side, :, a * 128 : (a + 1) * 128] = both[a][0:8]
        for a in range(half_tiles):
            b = tiles + a
            x_s[s, side, :, b * 128 : (b + 1) * 128] = both[a][8:16] + pltpu.roll(
                both[a + half_tiles][8:16], 4, 0)

    def unpack_x(s, side):
        def tile(a):
            return x_r[s, side, :, a * 128 : (a + 1) * 128]

        both = []
        for a in range(tiles):
            rest = tile(tiles + a % half_tiles)
            if a >= half_tiles:
                rest = pltpu.roll(rest, 4, 0)
            both.append(jnp.concatenate([tile(a), rest], axis=0))
        faces_of = []
        for c in range(comps):
            high = both[comps + c // 2]
            if c % 2:
                high = pltpu.roll(high, 64, 1)
            faces_of.append(jnp.concatenate([both[c], high], axis=1))
        return faces_of

    def couple(parts, s, before_sends=None):
        pieces = [split(p) for p in parts]
        acc = None
        inner = []
        x_faces = []
        for c, (hi, lo) in enumerate(pieces):
            t = bdot(mxy, jnp.concatenate([hi, hi, lo], axis=0))
            trace_s[s, :, c * BLK : (c + 1) * BLK] = t[nh + 32 : nh + 48]
            x_faces.append(t[nh : nh + 32])
            inner.append(t[:nh])
        pack_x([t[:16] for t in x_faces], s, 0)
        pack_x([t[16:] for t in x_faces], s, 1)
        if before_sends is not None:
            before_sends()
        for sends, _, copy in faces(s)[:4]:
            pl.when(sends)(copy.start)
        w = bdot(
            jnp.concatenate(
                [jnp.concatenate([p[h] for p in pieces], axis=0) for h in (0, 1, 0)], axis=1),
            kz)
        lanes = cols_of(128)
        for c in range(comps):
            wc = w[c * nh : (c + 1) * nh]
            keep = (lanes == nz - 128 + c) | (lanes == nz - 120 + c)
            piece = jnp.where(keep, wc[:, 128:256], 0.0)
            acc = piece if acc is None else acc + piece
            inner[c] = inner[c] + wc
        zsend_s[s] = acc
        for sends, _, copy in faces(s)[4:]:
            pl.when(sends)(copy.start)
        return inner

    def finish(s):
        for _, receives, copy in faces(s):
            pl.when(receives)(copy.wait_recv)

    def update(parts, inner, s):
        zn, zp = z_r[s, 0], z_r[s, 1]
        r = r_s[...]
        new = []
        below, above = unpack_x(s, 0), unpack_x(s, 1)
        for c in range(comps):
            sides = [below[c], above[c], halo_r[s, :, c * BLK : (c + 1) * BLK]]
            add = bdot(inj, right3(jnp.concatenate(sides, axis=0)))
            zlo = zp[:, nz - 120 + c : nz - 119 + c] * zin0
            zhi = zn[:, nz - 128 + c : nz - 127 + c] * zin5
            total = inner[c] + add + jnp.concatenate([zlo, zhi], axis=1)
            new.append((1.0 - OMEGA) * parts[c] + r * (f_s[c] + TAU * total))
        return new

    local[1].wait()
    state = forward(u_in)
    inner = couple(
        state, 0, lambda: pl.semaphore_wait(barrier, (n_fc - 1) + (n_row - 1)))
    for c in range(comps):
        u_s[c] = state[c]

    local[2].wait()
    local[3].wait()
    flat_s[...] = jnp.zeros(flat_s.shape, F32)
    for n in range(NT - 1):
        flat_s[n * 4 : (n + 1) * 4, 0:pan] = hist_ref[n]
    flat_s[64:67, 0:pan] = pts_ref[...]
    packed = flat_s[0:24]
    for g in (1, 2):
        packed = packed + pltpu.roll(flat_s[g * 24 : (g + 1) * 24], g * pan, 1)
    pan_s[...] = packed
    pan_r[row] = packed
    for d in range(1, n_row):
        pan_copy(d).start()

    local[4].wait()
    for c, part in enumerate(forward(f_in)):
        f_s[c] = part
    for i in (5, 6, 7):
        local[i].wait()
    on_q = where01(rows_of(ez) == zqc).astype(BF16)
    lam2 = sum(bdot(p, on_q) for p in split(lam_ref[0]))
    den = lookup(vals_ref[0:1], ir) + lookup(vals_ref[1:2], jr) + lookup(vals_ref[2:3], zkc)
    for e in range(ey):
        den = den + where01(er == e) * lam2[e : e + 1]
    r_s[...] = jnp.where(inside, OMEGA / jnp.where(inside, den, 1.0), 0.0)

    a_back = pick(sx, nr, ic) * pick(sy, mjr, jc) * where01((mer == ec) & (myr < ny))
    a_back = left3(a_back)
    z_back = right3(pick(sz, zkr, zkc, True) * where01((zqr == zqc) & inside))
    zs = cols_of(128) - (row * pan).astype(F32)
    sq, sk = divmod_of(zs, N)
    z_new = pick(sz, zkr, sk, True) * where01((zqr == sq) & (zs >= 0) & (zs < pan))
    z_new = right3(z_new)
    own = where01(cols_of(n_obs) == rows_of(own_obs) + (row * own_obs).astype(F32))
    mine = ddot(own, obs_ref[...], NTD)
    half, freq = divmod_of(rows_of(2 * NF), NF)
    time, chan = divmod_of(cols_of(4 * NT), 4)
    sin_t, cos_t = sincos((freq + 0.5) * (math.pi / NF) * time)
    table = jnp.where(half == 0, cos_t, -sin_t)
    last = table[:, 4 * NT - 1 : 4 * NT]
    wide = jnp.concatenate([table * where01(chan == c) for c in range(4)], axis=0)

    finish(0)
    state = update([u_s[c] for c in range(comps)], inner, 0)
    inner = couple(state, 1)
    for c in range(comps):
        u_s[c] = state[c]

    for d in range(1, n_row):
        pan_wait(d)
    groups = []
    for g in range(3):
        group = jnp.zeros((24, 128), F32)
        for i in range(n_row):
            shift = ((i - g) * pan) % 128
            moved = pan_r[i] if shift == 0 else pltpu.roll(pan_r[i], shift, 1)
            here = (cols_of(128) >= i * pan) & (cols_of(128) < (i + 1) * pan)
            group = jnp.where(here, moved, group)
        groups.append(group)
    panels = jnp.concatenate(groups, axis=0)
    dx, dy, dz = (mine[:, a : a + 1] - panels[64 + a : 65 + a, :] for a in range(3))
    r2 = dx * dx + dy * dy + dz * dz
    radius = jnp.sqrt(r2)
    inv = 1.0 / radius
    dx, dy, dz = dx * inv, dy * inv, dz * inv
    amp = inv * (1.0 / (4.0 * math.pi))
    step = KMAX / NF
    sin_r, ar = sincos(radius * (0.5 * step))
    ai = -sin_r
    sr, si = ar * ar - ai * ai, 2.0 * ar * ai
    ar, ai = ar * amp, ai * amp
    spectral = ddot(wide, panels[0:64])
    lane128 = lax.broadcasted_iota(jnp.int32, (1, 128), 1)
    total = jnp.zeros((own_obs, 128), F32)
    for f in range(NF):
        k = step * (f + 0.5)
        er_s[f], ei_s[f] = ar, ai
        re = [spectral[2 * NF * c + f : 2 * NF * c + f + 1] for c in range(4)]
        im = [spectral[2 * NF * c + NF + f : 2 * NF * c + NF + f + 1] for c in range(4)]
        d_re = dx * re[1] + dy * re[2] + dz * re[3]
        d_im = dx * im[1] + dy * im[2] + dz * im[3]
        t_re = d_re * inv - k * (im[0] + d_im)
        t_im = d_im * inv + k * (re[0] + d_re)
        s_re = jnp.sum(ar * t_re - ai * t_im, axis=1, keepdims=True)
        s_im = jnp.sum(ar * t_im + ai * t_re, axis=1, keepdims=True)
        total = jnp.where(lane128 == f, s_re, total)
        total = jnp.where(lane128 == NF + f, s_im, total)
        if f < NF - 1:
            ar, ai = ar * sr - ai * si, ar * si + ai * sr

    finish(1)
    state = update([u_s[c] for c in range(comps)], inner, 1)
    pieces = [split(p) for p in state]
    corners = jnp.zeros((8, BLK), F32)
    for c in range(4):
        hi, lo = pieces[c]
        top = bdot(a_back[0:16], jnp.concatenate([hi, hi, lo], axis=0))[0:1]
        corners = jnp.where(t8 == c, top, corners)
    new_s[...] = bdot(left3(corners), z_new)
    for d in range(1, n_row):
        new_copy(d).start()

    w = bdot(
        jnp.concatenate(
            [jnp.concatenate([p[h] for p in pieces], axis=0) for h in (0, 1, 0)], axis=1),
        z_back)
    for c in range(comps):
        nodes = bdot(a_back, right3(w[c * nh : (c + 1) * nh]))
        for i in range(nx):
            out_buf[c, i] = nodes[i * 16 : i * 16 + ny, :nz]
    out_copy = pltpu.make_async_copy(out_buf, out_hbm, local_sem.at[8])
    out_copy.start()

    for d in range(1, n_row):
        new_copy(d).wait_recv()
    newest = new_s[...]
    for d in range(1, n_row):
        newest = newest + new_r[d]
    along = dx * newest[1:2] + dy * newest[2:3] + dz * newest[3:4]
    a_val = newest[0:1] + along
    b_val = along * inv
    fresh = jnp.zeros((own_obs, 128), F32)
    for f in range(NF):
        k = step * (f + 0.5)
        ka = k * a_val
        gr, gi = er_s[f], ei_s[f]
        s_re = jnp.sum(gr * b_val - gi * ka, axis=1, keepdims=True)
        s_im = jnp.sum(gr * ka + gi * b_val, axis=1, keepdims=True)
        fresh = jnp.where(lane128 == f, s_re, fresh)
        fresh = jnp.where(lane128 == NF + f, s_im, fresh)
    turned = jnp.concatenate([fresh, total], axis=0).T
    fr, fi = turned[0:NF], turned[NF : 2 * NF]
    c15, s15 = last[0:NF], last[NF : 2 * NF]
    part_re = c15 * fr - s15 * fi + pltpu.roll(fr, own_obs, 1)
    part_im = c15 * fi + s15 * fr + pltpu.roll(fi, own_obs, 1)
    part = jnp.where(lane128 < own_obs, part_re, pltpu.roll(part_im, own_obs, 1))
    part_s[...] = part
    part_r[fc] = part
    each_fc(lambda d: part_copy(d).start())
    each_fc(part_wait)
    if n_fc <= 16:
        spectra = part_r[0]
        for d in range(1, n_fc):
            spectra = spectra + part_r[d]
    else:
        spectra = lax.fori_loop(1, n_fc, lambda d, acc: acc + part_r[d], part_r[0])
    spec_ref[0] = spectra[:, :own_obs]
    spec_ref[1] = spectra[:, own_obs : 2 * own_obs]

    for s in range(SWEEPS):
        for sends, _, copy in faces(s):
            pl.when(sends)(copy.wait_send)
    for d in range(1, n_row):
        pan_copy(d).wait_send()
        new_copy(d).wait_send()
    each_fc(lambda d: part_copy(d).wait_send())
    out_copy.wait()


def on_device(forcing, previous, shift, bases, values, observers, points, history):
    n_flow, n_col, n_row = (lax.axis_size(a) for a in ("flow", "col", "row"))
    comps, nx, ny, nz = forcing.shape
    n_fc = n_flow * n_col
    pan = points.shape[1]
    n_obs = observers.shape[1]
    own_obs = n_obs // n_row
    nh = -(-nx * ny // 16) * 16
    sizes = (n_flow, n_col, n_row, comps, nx, ny, nz, pan, n_obs, nh)
    tiles = 2 * -(-(comps + (comps + 1) // 2) // 2)
    history = jnp.transpose(history, (1, 0, 2))
    vmem = pl.BlockSpec(memory_space=pltpu.VMEM)
    hbm = pl.BlockSpec(memory_space=pl.ANY)
    dma = pltpu.SemaphoreType.DMA
    return pl.pallas_call(
        functools.partial(kernel, sizes),
        out_shape=(
            jax.ShapeDtypeStruct(forcing.shape, F32),
            jax.ShapeDtypeStruct((2, NF, own_obs), F32),
        ),
        in_specs=[pl.BlockSpec(memory_space=pltpu.HBM)] * 8,
        out_specs=(hbm, vmem),
        scratch_shapes=[
            pltpu.VMEM((comps, nx, ny, nz), F32),
            pltpu.VMEM((comps, nx, ny, nz), F32),
            pltpu.VMEM(shift.shape, F32),
            pltpu.VMEM(bases.shape, F32),
            pltpu.VMEM(values.shape, F32),
            pltpu.VMEM(observers.shape, F32),
            pltpu.VMEM(points.shape, F32),
            pltpu.VMEM(history.shape, F32),
            pltpu.VMEM((comps, nx, ny, nz), F32),
            pltpu.VMEM((comps, nh, BLK), F32),
            pltpu.VMEM((comps, nh, BLK), F32),
            pltpu.VMEM((nh, BLK), F32),
            pltpu.VMEM((SWEEPS, 2, 8, tiles * 192), F32),
            pltpu.VMEM((SWEEPS, 2, 8, tiles * 192), F32),
            pltpu.VMEM((SWEEPS, 16, comps * BLK), F32),
            pltpu.VMEM((SWEEPS, nh, 128), F32),
            pltpu.VMEM((SWEEPS, 16, comps * BLK), F32),
            pltpu.VMEM((SWEEPS, 2, nh, 128), F32),
            pltpu.VMEM((72, 128), F32),
            pltpu.VMEM((24, 128), F32),
            pltpu.VMEM((n_row, 24, 128), F32),
            pltpu.VMEM((8, 128), F32),
            pltpu.VMEM((n_row, 8, 128), F32),
            pltpu.VMEM((NF, own_obs, 128), F32),
            pltpu.VMEM((NF, own_obs, 128), F32),
            pltpu.VMEM((NF, 128), F32),
            pltpu.VMEM((n_fc, NF, 128), F32),
            dma((9,)),
            dma((SWEEPS, 6)),
            dma((SWEEPS, 6)),
            dma((n_row,)),
            dma((n_row,)),
            dma((n_row,)),
            dma((n_row,)),
            dma((n_fc,)),
            dma((n_fc,)),
        ],
        compiler_params=pltpu.CompilerParams(
            collective_id=0, has_side_effects=True, vmem_limit_bytes=60 * 1024 * 1024
        ),
    )(forcing, previous, shift, bases, values, observers, points, history)


def solution(mesh):
    return jax.shard_map(
        on_device,
        mesh=mesh,
        in_specs=(
            P(None, "flow", "col", "row"),
            P(None, "flow", "col", "row"),
            P("flow", "col", "row"),
            P(),
            P(),
            P(),
            P(None, ("flow", "col", "row")),
            P(None, None, ("flow", "col", "row")),
        ),
        out_specs=(P(None, "flow", "col", "row"), P(None, None, "row")),
        check_vma=False,
    )
```
